32 devices in a mesh: slab: 2 (over y), orb: 16 (over z, x, core).
Axes of the slice: x: 2, y: 2, z: 4, core: 2. Of those that a mesh axis runs over, the one named last changes fastest.
Arguments:
- orbitals_t: bfloat16 [2048, 16384], P('orb', 'slab'), may hold values from -6 to 6
- tiles: bfloat16 [224, 128, 128], P('slab'), may hold values from -0.375 to 0.375
- tile_rows: int32 [224], P('slab'), may hold values from 0 to 63
- tile_cols: int32 [224], P('slab'), may hold values from -2 to 65, as said below
- row_counts: int32 [128], P('slab'), may hold values from 1 to 128, 12288 in all
- bounds: float32 [3], replicated, may hold values from 0 to 1
- rotation: bfloat16 [2048, 2048], P('orb'), may hold values from -0.125 to 0.125
Outputs:
- rotated_t: bfloat16 [2048, 16384], P('orb', 'slab')
The draws below stay inside these ranges and needn't reach their ends.
Inputs may be any that keep to these rules, and one draw needn't show every extreme that they name: `tile_cols`: within every slab, the first 64 tiles are the diagonal tiles of row blocks 0 to 63 in order; a tile's column block lies within 2 blocks of its row block; in every slab some tile of row block 0 has column block -2 and some tile of row block 63 has column block 65.
All inputs are finite; a program needn't handle non-finite values. No bound on the sum of `row_counts` on one device may be relied on, other than what follows from the above.
Results may differ from the reference program's by a relative error of at most 0.006.
Values may be sent and summed in bfloat16 or wider, within the bound.
No kernel may reach another device: no remote copies, remote signals or barrier semaphores. Data moves between devices by JAX's collectives and lax.ppermute only.
A program may use at most 64 MiB of HBM per device.

```python
import math
import jax
import jax.numpy as jnp
import numpy as np
from jax import lax

NORB = 2048
TILE = 128
HB = 2
BLK_SLAB = 64
TILES_SLAB = 112
NBLK = 128
ROWS = 16384
N_SLAB = 2


def tile_layout(key):
    key_one, key_two, key_three, key_four = jax.random.split(jax.random.fold_in(key, 7), 4)
    extra = TILES_SLAB - BLK_SLAB
    extra_rows = jax.random.randint(key_one, (N_SLAB, extra), 0, BLK_SLAB)
    magnitude = jax.random.randint(key_two, (N_SLAB, extra), 1, HB + 1)
    signs = jax.random.randint(key_three, (N_SLAB, extra), 0, 2) * 2 - 1
    offsets = magnitude * signs
    extra_rows = extra_rows.at[:, 0].set(0).at[:, 1].set(BLK_SLAB - 1)
    offsets = offsets.at[:, 0].set(-HB).at[:, 1].set(HB)
    extra_cols = extra_rows + offsets
    slab_keys = jax.random.split(key_four, N_SLAB)
    orders = jax.vmap(lambda one_key: jax.random.permutation(one_key, extra))(slab_keys)
    extra_rows = jnp.take_along_axis(extra_rows, orders, axis=1)
    extra_cols = jnp.take_along_axis(extra_cols, orders, axis=1)
    diagonal = jnp.broadcast_to(jnp.arange(BLK_SLAB, dtype=jnp.int32), (N_SLAB, BLK_SLAB))
    row_lists = jnp.concatenate([diagonal, extra_rows.astype(jnp.int32)], axis=1)
    col_lists = jnp.concatenate([diagonal, extra_cols.astype(jnp.int32)], axis=1)
    return (row_lists.reshape(-1), col_lists.reshape(-1))


def draw_tile_rows(key, part):
    return tile_layout(key)[0]


def draw_tile_cols(key, part):
    return tile_layout(key)[1]


def level_of(stream_key, dims, shards, least, top_value):
    def one(axis_at, parts):
        steps = jax.random.uniform(jax.random.fold_in(jax.random.fold_in(stream_key, 6), axis_at), (parts,), jnp.float32, least / len(shards), top_value / len(shards))
        return jnp.repeat(jnp.exp(steps), dims[axis_at] // parts).reshape((-1,) + (1,) * (len(dims) - axis_at - 1))

    factor_of = one(*shards[0])
    for cut in shards[1:]:
        factor_of = factor_of * one(*cut)
    return factor_of


def length_profile(number_of, total, bound, slope):
    portions = [(1 << 20) // math.isqrt(standing ** slope) + 1 for standing in range(2, number_of + 1)]
    spare, given = total - bound - (number_of - 1), [1] * (number_of - 1)
    while spare > 0:
        free = [i for i in range(number_of - 1) if given[i] < bound]
        mass, budget = sum([portions[i] for i in free]), spare
        for i in free:
            more = min(bound - given[i], max(1, budget * portions[i] // mass), spare)
            given[i] = given[i] + more
            spare = spare - more
    return np.array([bound] + given)


def ragged(key, number_of, total, bound, skew):
    if number_of == 2:
        one = jax.random.randint(key, (), max(1, total - bound), min(bound, total - 1) + 1)
        return jnp.stack([one, total - one])
    sizes = jnp.asarray(length_profile(number_of, total, bound, skew), jnp.int32)
    pairs = (number_of - 1) // 2
    giver, sink = sizes[1:1 + 2 * pairs:2], sizes[2:2 + 2 * pairs:2]
    room = jnp.minimum(giver - 1, bound - sink)
    moved = jax.random.randint(jax.random.fold_in(key, 1), (pairs,), 0, 1 << 20) % (room + 1)
    sizes = sizes.at[1:1 + 2 * pairs:2].set(giver - moved).at[2:2 + 2 * pairs:2].set(sink + moved)
    return sizes[jax.random.permutation(jax.random.fold_in(key, 2), number_of)]


def gaussian(key, dims, deviation, bound, cuts=(), kind=jnp.bfloat16):
    gain = level_of(key, dims, cuts, -0.22, 0.18) if cuts else 1.0
    drawn = jax.random.normal(key, dims, jnp.float32) * deviation * gain
    return jnp.minimum(jnp.maximum(drawn, -bound), bound).astype(kind)


def setup_inputs(seed: int = 0) -> dict:
    keys = jax.random.split(jax.random.key(seed), 8)
    orbitals_t = gaussian(keys[0], (NORB, ROWS), 1.0, 6.0, ((0, 16), (1, 2)))
    tiles = gaussian(keys[1], (N_SLAB * TILES_SLAB, TILE, TILE), (2 * TILE) ** -0.5, 0.375, ((0, 2),))
    tile_rows = draw_tile_rows(jax.random.fold_in(keys[7], 71), 0)
    tile_cols = draw_tile_cols(jax.random.fold_in(keys[7], 71), 0)
    row_counts = ragged(keys[4], NBLK, NBLK * TILE * 3 // 4, TILE, 2).astype(jnp.int32)
    bounds = jnp.clip(jax.random.uniform(keys[5], (3,), jnp.float32, 0.0, 1.0), 0.0, 1.0)
    rotation = gaussian(keys[6], (NORB, NORB), NORB ** -0.5, 0.125, ((0, 16),))
    return dict(orbitals_t=orbitals_t, tiles=tiles, tile_rows=tile_rows, tile_cols=tile_cols, row_counts=row_counts, bounds=bounds, rotation=rotation)


def tile_product(source, tiles, tile_rows, tile_cols):
    col_blocks = source.reshape(NORB, NBLK, TILE)
    col_blocks = jnp.pad(col_blocks, ((0, 0), (HB, HB), (0, 0)))
    row_lists = tile_rows.reshape(N_SLAB, TILES_SLAB)
    col_lists = tile_cols.reshape(N_SLAB, TILES_SLAB)
    slab_tiles = tiles.reshape(N_SLAB, TILES_SLAB, TILE, TILE)

    def one_slab(slab_index):
        where = slab_index * BLK_SLAB + col_lists[slab_index] + HB
        picked = jnp.take(col_blocks, where.astype(jnp.int32), axis=1).astype(jnp.float32)
        products = jnp.einsum('otc,trc->otr', picked, slab_tiles[slab_index].astype(jnp.float32))
        onehot = (row_lists[slab_index][:, None] == jnp.arange(BLK_SLAB, dtype=jnp.int32)[None, :]).astype(jnp.float32)
        return jnp.einsum('otr,tb->obr', products, onehot, precision=lax.Precision.HIGHEST)

    summed = lax.map(one_slab, jnp.arange(N_SLAB, dtype=jnp.int32))
    return jnp.transpose(summed, (1, 0, 2, 3)).reshape(NORB, ROWS)


def reference(orbitals_t, tiles, tile_rows, tile_cols, row_counts, bounds, rotation):
    lower_bound = -3.0 + bounds[0]
    cutoff = bounds[1] - 0.5
    upper_bound = 3.0 + bounds[2]
    half_width = (upper_bound - cutoff) / 2.0
    center = (upper_bound + cutoff) / 2.0
    sigma_one = half_width / (lower_bound - center)
    sigma_two = 1.0 / (2.0 / sigma_one - sigma_one)
    live = (jnp.arange(TILE, dtype=jnp.int32)[None, :] < row_counts[:, None]).astype(jnp.float32).reshape(ROWS)
    source = orbitals_t.astype(jnp.float32)
    applied = tile_product(orbitals_t, tiles, tile_rows, tile_cols)
    filtered_one = (live * (applied - center * source) * (sigma_one / half_width)).astype(jnp.bfloat16)
    applied = tile_product(filtered_one, tiles, tile_rows, tile_cols)
    first = filtered_one.astype(jnp.float32)
    filtered_two = (live * ((applied - center * first) * (2.0 * sigma_two / half_width) - sigma_one * sigma_two * source)).astype(jnp.bfloat16)
    rotated = jnp.dot(rotation.T, filtered_two, preferred_element_type=jnp.float32)
    return rotated.astype(jnp.bfloat16)
```

```python
import functools

import jax
import jax.numpy as jnp
from jax import lax
from jax.experimental import pallas as pl
from jax.experimental.pallas import tpu as pltpu
from jax.sharding import PartitionSpec as P

HB = 2
EDGE = 2 * HB
PLANE = 4
VMEM = pl.BlockSpec(memory_space=pltpu.VMEM)
SMEM = pl.BlockSpec(memory_space=pltpu.SMEM)
COST = pl.CostEstimate(flops=1000, bytes_accessed=1000, transcendentals=0)
PARAMS = pltpu.CompilerParams(vmem_limit_bytes=36 * 1024 * 1024)
f32, bf16 = jnp.float32, jnp.bfloat16


def call(body, out_shape, in_specs, scratch_shapes=()):
    return pl.pallas_call(
        body,
        out_shape=out_shape,
        in_specs=in_specs,
        out_specs=jax.tree.map(lambda _: VMEM, out_shape),
        scratch_shapes=scratch_shapes,
        compiler_params=PARAMS,
        cost_estimate=COST,
    )


def after(value, *done):
    return lax.optimization_barrier((value, done))[0]


def coefficients(bounds_ref):
    lower_bound = -3.0 + bounds_ref[0]
    cutoff = bounds_ref[1] - 0.5
    upper_bound = 3.0 + bounds_ref[2]
    half_width = (upper_bound - cutoff) / 2.0
    center = (upper_bound + cutoff) / 2.0
    sigma_one = half_width / (lower_bound - center)
    sigma_two = 1.0 / (2.0 / sigma_one - sigma_one)
    return center, sigma_one / half_width, 2.0 * sigma_two / half_width, sigma_one * sigma_two


def loop(start, stop, body, unroll, carry=0):
    return lax.fori_loop(start, stop, body, carry, unroll=unroll)


def product(tile, block):
    return jnp.dot(tile, block, preferred_element_type=f32)


def is_edge(row, blocks):
    return (row < HB) | (row >= blocks - HB)


def edge_slot(row, blocks):
    return jnp.where(row < HB, row, row - blocks + EDGE)


def edge_row(slot, blocks):
    return slot if slot < HB else blocks - EDGE + slot


def live_mask(tile, lanes, count):
    return lax.broadcasted_iota(jnp.int32, (tile, lanes), 0) < count


def sum_counts(counts_ref, rows):
    total = 0
    for r in rows:
        total = total + counts_ref[r]
    return total


def start_kernel(groups, place_ref, x_ref, rotation_ref, halo_ref, *piece_refs):
    width = halo_ref.shape[1]
    z, slab, p = place_ref[0], place_ref[1], place_ref[2]
    begin = jnp.where(slab == 0, x_ref.shape[1] - width, 0)
    halo_ref[...] = x_ref[:, pl.ds(pl.multiple_of(begin, width), width)]
    lanes = piece_refs[0].shape[1] // groups
    half = groups // 2
    for q, ref in enumerate(piece_refs):
        for h in range(2):
            for g in range(half):
                block = ((slab ^ h) * half + g) * PLANE + (p ^ q)
                begin = pl.multiple_of(block * lanes, lanes)
                ref[:, (h * half + g) * lanes:(h * half + g + 1) * lanes] = rotation_ref[
                    :, pl.ds(begin, lanes)
                ]


def multiply(blocks, rows_ref, cols_ref, tiles_ref, source_ref, acc_ref, extra_ref, first=None):
    def diagonal(r, _):
        block = source_ref[r] if first is None else first(r)
        acc_ref[r] = product(tiles_ref[r], block)
        return 0

    loop(0, blocks, diagonal, 16)
    listed = tiles_ref.shape[0]

    def extra(k, _):
        col = jnp.clip(cols_ref[k], 0, blocks - 1)
        extra_ref[k - blocks] = product(tiles_ref[k], source_ref[col])
        return 0

    loop(blocks, listed, extra, 16)

    def gather(k, _):
        @pl.when((cols_ref[k] >= 0) & (cols_ref[k] < blocks))
        def _():
            acc_ref[rows_ref[k]] += extra_ref[k - blocks]

        return 0

    loop(blocks, listed, gather, 4)


def multiply_edges(blocks, slab, rows_ref, cols_ref, tiles_ref, halo_ref, add):
    def extra(k, _):
        col = cols_ref[k]
        slot = jnp.where(slab == 0, col - blocks, col + HB)

        @pl.when(((col < 0) | (col >= blocks)) & (slot >= 0) & (slot < HB))
        def _():
            add(rows_ref[k], product(tiles_ref[k], halo_ref[slot]))

        return 0

    loop(blocks, tiles_ref.shape[0], extra, 4)


def first_kernel(
    blocks, place_ref, rows_ref, cols_ref, counts_ref, bounds_ref, x_ref, halo_ref, tiles_ref,
    f1_ref, edge_ref, xt_ref, acc_ref, extra_ref, ext_ref,
):
    tile = tiles_ref.shape[1]
    lanes = x_ref.shape[0]
    slab = place_ref[1]

    def turn(r):
        xt_ref[r] = x_ref[:, pl.ds(pl.multiple_of(r * tile, tile), tile)].T
        return xt_ref[r]

    multiply(blocks, rows_ref, cols_ref, tiles_ref, xt_ref, acc_ref, extra_ref, turn)
    for b in range(HB):
        ext_ref[b] = halo_ref[:, b * tile:(b + 1) * tile].T

    def add(row, value):
        acc_ref[row] += value

    multiply_edges(blocks, slab, rows_ref, cols_ref, tiles_ref, ext_ref, add)
    center, scale = coefficients(bounds_ref)[:2]

    def finish(r, _):
        value = (acc_ref[r] - center * xt_ref[r].astype(f32)) * scale
        f1_ref[r] = jnp.where(live_mask(tile, lanes, counts_ref[r]), value, 0.0).astype(bf16)
        return 0

    loop(0, blocks, finish, 4)
    begin = jnp.where(slab == 0, blocks - HB, 0)
    for b in range(HB):
        edge_ref[b] = f1_ref[begin + b]


def second_values(r, acc, block, xt_ref, counts_ref, scales):
    tile, lanes = block.shape
    center, _, scale, both = scales
    value = (acc - center * block.astype(f32)) * scale - both * xt_ref[r].astype(f32)
    return jnp.where(live_mask(tile, lanes, counts_ref[r]), value, 0.0)


def split_parts(outs, place_ref, packed_ref, base):
    part = outs[0].shape[0]
    for s, out in enumerate(outs):
        start = pl.multiple_of(base + (place_ref[0] ^ s) * part, 16)
        out[...] = packed_ref[pl.ds(start, part)].astype(bf16)


def second_kernel(
    blocks, groups, place_ref, rows_ref, cols_ref, counts_ref, bounds_ref, f1_ref, xt_ref, tiles_ref,
    *refs,
):
    outs, refs = refs[:groups], refs[groups:]
    shared_ref, excess_ref, rest_ref, edge_ref, acc_ref, extra_ref, packed_ref = refs
    tile = tiles_ref.shape[1]
    multiply(blocks, rows_ref, cols_ref, tiles_ref, f1_ref, acc_ref, extra_ref)
    edges = [edge_row(e, blocks) for e in range(EDGE)]
    for e, r in enumerate(edges):
        edge_ref[e] = acc_ref[r]
    scales = coefficients(bounds_ref)

    def finish(r, offset):
        packed_ref[pl.ds(offset, tile)] = second_values(
            r, acc_ref[r], f1_ref[r], xt_ref, counts_ref, scales
        )
        return offset + counts_ref[r]

    loop(HB, blocks - HB, finish, 4, sum_counts(counts_ref, edges))
    size = rest_ref.shape[0]
    rest_ref[...] = packed_ref[:size]
    split_parts(outs, place_ref, packed_ref, size)
    shared_ref[...] = packed_ref[2 * size:3 * size].astype(bf16)
    excess_ref[...] = packed_ref[3 * size:4 * size].astype(bf16)


def second_edge_kernel(
    blocks, groups, place_ref, rows_ref, cols_ref, counts_ref, bounds_ref, halo_ref, f1_ref, xt_ref,
    tiles_ref, sum_ref, rest_ref, *refs,
):
    outs, (acc_ref, packed_ref) = refs[:groups], refs[groups:]
    tile = tiles_ref.shape[1]
    acc_ref[...] = sum_ref[...]

    def add(row, value):
        acc_ref[edge_slot(row, blocks)] += value

    multiply_edges(blocks, place_ref[1], rows_ref, cols_ref, tiles_ref, halo_ref, add)
    scales = coefficients(bounds_ref)
    packed_ref[...] = rest_ref[...]
    offset = 0
    for e in range(EDGE):
        r = edge_row(e, blocks)
        value = second_values(r, acc_ref[e], f1_ref[r], xt_ref, counts_ref, scales)
        here = pl.ds(offset, tile)
        live = live_mask(tile, value.shape[1], counts_ref[r])
        packed_ref[here] = jnp.where(live, value, packed_ref[here])
        offset = offset + counts_ref[r]
    split_parts(outs, place_ref, packed_ref, 0)


def merge_kernel(blocks, groups, place_ref, counts_ref, shared_ref, excess_ref, *refs):
    outs, packed_ref = refs[:groups], refs[groups]
    size = shared_ref.shape[0]
    live = sum_counts(counts_ref, range(blocks))
    packed_ref[:size] = shared_ref[...].astype(f32)
    packed_ref[pl.ds(jnp.clip(live - 2 * size, 0, size), size)] = excess_ref[...].astype(f32)
    split_parts(outs, place_ref, packed_ref, 0)


def rotate_kernel(groups, place_ref, *refs):
    own, over_x, over_core, over_both = refs[:4]
    mine, near, far_two, far_three, other_two, other_three = refs[4:10]
    outs, turned = refs[10:10 + groups], refs[-1]
    width = outs[0].shape[1]
    half = groups // 2 * width
    lhs = jnp.concatenate(
        [ref[s] for s in range(groups) for ref in (own, over_core, over_x, over_both)], axis=1
    )
    for h in range(2):
        far = (far_two, far_three) if h == 0 else (other_two, other_three)
        rhs = [ref[:, h * half:(h + 1) * half] for ref in (mine, near)] + [ref[...] for ref in far]
        total = product(lhs, jnp.concatenate(rhs, axis=0)).astype(bf16)
        first = (place_ref[1] ^ h) * (groups // 2)
        for z in range(groups // 2):
            turned[first + z] = total[:, z * width:(z + 1) * width]
    for s in range(groups):
        outs[s][...] = turned[place_ref[0] ^ s]


def spread_kernel(blocks, groups, place_ref, counts_ref, back_ref, *refs):
    parts, out_ref, packed_ref = refs[:-2], refs[-2], refs[-1]
    part, width = parts[0].shape
    size = part * groups
    tile = out_ref.shape[1] // blocks
    live = sum_counts(counts_ref, range(blocks))
    packed_ref[pl.ds(jnp.clip(live - size, 2 * size, 3 * size), size)] = back_ref[...].astype(f32)
    for i in range(3):
        for s in range(groups):
            start = pl.multiple_of((i * groups + (place_ref[0] ^ s)) * part, 16)
            packed_ref[pl.ds(start, part)] = parts[i * groups + s][...].astype(f32)

    def one(b, offset):
        rows = packed_ref[pl.ds(offset, tile)]
        rows = jnp.where(live_mask(tile, width, counts_ref[b]), rows, 0.0)
        out_ref[:, pl.ds(pl.multiple_of(b * tile, tile), tile)] = rows.T.astype(bf16)
        return offset + counts_ref[b]

    offset = 0
    for e in range(EDGE):
        offset = one(edge_row(e, blocks), offset)
    loop(HB, blocks - HB, one, 4, offset)


def paired(orbitals_t, tiles, tile_rows, tile_cols, row_counts, bounds, rotation):
    norb_dev, rows_dev = orbitals_t.shape
    listed, tile = tiles.shape[:2]
    blocks = rows_dev // tile
    orbs = lax.axis_size("orb")
    groups = orbs // PLANE
    me, slab = lax.axis_index("orb"), lax.axis_index("slab")
    z, p = me // PLANE, me % PLANE
    place = jnp.stack([z, slab, p])
    size = rows_dev // 4
    part = size // groups
    block_shape = (blocks, tile, norb_dev)
    edge_shape = (EDGE, tile, norb_dev)
    halo_shape = (HB, tile, norb_dev)
    extra_shape = (listed - blocks, tile, norb_dev)
    size_shape = (size, norb_dev)
    lists = (place, tile_rows, tile_cols, row_counts, bounds)

    def shaped(shape, dtype=bf16):
        return jax.ShapeDtypeStruct(shape, dtype)

    part_outs = [shaped((part, norb_dev))] * groups

    def swap(value, bits):
        return lax.ppermute(value, "orb", [(i, i ^ bits) for i in range(orbs)])

    def over_z(values):
        moved = {s: swap(values[s], s * PLANE) for s in (2, 3, 1)}
        return [values[0], moved[1], moved[2], moved[3]]

    def other_slab(value):
        return lax.ppermute(value, "slab", [(0, 1), (1, 0)])

    half = groups // 2 * norb_dev
    halo, *pieces = call(
        functools.partial(start_kernel, groups),
        [shaped((norb_dev, HB * tile))] + [shaped((norb_dev, 2 * half))] * PLANE,
        [SMEM] + [VMEM] * 2,
    )(place, orbitals_t, rotation)
    halo = other_slab(halo)
    mine = [pieces[0]] + [swap(pieces[q], q) for q in range(1, PLANE)]
    mine = jnp.concatenate(mine, axis=0)
    far_two = swap(mine[:, :half], 2 * PLANE)
    near = swap(mine, PLANE)

    f1, edge, xt = call(
        functools.partial(first_kernel, blocks),
        [shaped(block_shape), shaped(halo_shape), shaped(block_shape)],
        [SMEM] * 5 + [VMEM] * 3,
        [pltpu.VMEM(block_shape, f32), pltpu.VMEM(extra_shape, f32), pltpu.VMEM(halo_shape, bf16)],
    )(*lists, orbitals_t, halo, tiles)
    halo = other_slab(edge)

    *first_parts, shared, excess, rest, edge_sum = call(
        functools.partial(second_kernel, blocks, groups),
        part_outs
        + [shaped(size_shape)] * 2 + [shaped(size_shape, f32), shaped(edge_shape, f32)],
        [SMEM] * 5 + [VMEM] * 3,
        [
            pltpu.VMEM(block_shape, f32),
            pltpu.VMEM(extra_shape, f32),
            pltpu.VMEM((rows_dev + tile, norb_dev), f32),
        ],
    )(*lists, after(f1, far_two), xt, tiles)
    excess = other_slab(excess)
    whole_first = over_z(first_parts)
    rest_parts = call(
        functools.partial(second_edge_kernel, blocks, groups),
        part_outs,
        [SMEM] * 5 + [VMEM] * 6,
        [pltpu.VMEM(edge_shape, f32), pltpu.VMEM(size_shape, f32)],
    )(*lists, halo, f1, xt, tiles, edge_sum, after(rest, near))
    shared = after(shared, rest_parts)
    shared_parts = call(
        functools.partial(merge_kernel, blocks, groups),
        part_outs,
        [SMEM] * 2 + [VMEM] * 2,
        [pltpu.VMEM((2 * size, norb_dev), f32)],
    )(place, row_counts, shared, excess)
    far_three = swap(far_two, PLANE)
    shared_parts = after(shared_parts, whole_first, far_three)
    weights = [mine, near, far_two, far_three, other_slab(far_two), other_slab(far_three)]

    def gather(whole):
        own = jnp.stack(whole)
        over_x = swap(own, 2)
        return own, over_x, swap(own, 1), swap(over_x, 1)

    def rotate(gathered):
        return call(
            functools.partial(rotate_kernel, groups),
            part_outs,
            [SMEM] + [VMEM] * (4 + len(weights)),
            [pltpu.VMEM((groups, part, norb_dev), bf16)],
        )(place, *gathered, *weights)

    whole_shared = over_z(shared_parts)
    whole_rest = over_z(after(rest_parts, whole_shared))
    whole_shared, weights = lax.optimization_barrier((whole_shared, weights))
    first_back = over_z(rotate(gather(whole_first)))
    shared_back = over_z(after(rotate(gather(whole_shared)), first_back))
    rest_back = over_z(after(rotate(gather(whole_rest)), shared_back))
    back = jnp.concatenate([jnp.zeros_like(v) for v in shared_back])
    for s, v in enumerate(shared_back):
        back = lax.dynamic_update_slice_in_dim(back, v, (z ^ s) * part, 0)
    back = other_slab(back)

    returned = rest_back + first_back + shared_back
    return call(
        functools.partial(spread_kernel, blocks, groups),
        shaped((norb_dev, rows_dev)),
        [SMEM] * 2 + [VMEM] * (1 + len(returned)),
        [pltpu.VMEM((rows_dev + 2 * tile, norb_dev), f32)],
    )(place, row_counts, back, *returned)


def with_halo(block, sides, width):
    for axis, dim in sides:
        count = lax.axis_size(axis)
        forward = [(i, i + 1) for i in range(count - 1)]
        backward = [(target, source) for source, target in forward]
        low = lax.ppermute(
            lax.slice_in_dim(block, block.shape[dim] - width, None, axis=dim), axis, forward
        )
        high = lax.ppermute(lax.slice_in_dim(block, 0, width, axis=dim), axis, backward)
        block = jnp.concatenate([low, block, high], axis=dim)
    return block


def general(orbitals_t, tiles, tile_rows, tile_cols, row_counts, bounds, rotation):
    norb_dev, rows_dev = orbitals_t.shape
    tile_size = tiles.shape[1]
    blocks = rows_dev // tile_size
    lower_bound = -3.0 + bounds[0]
    cutoff = bounds[1] - 0.5
    upper_bound = 3.0 + bounds[2]
    half_width = (upper_bound - cutoff) / 2.0
    center = (upper_bound + cutoff) / 2.0
    sigma_one = half_width / (lower_bound - center)
    sigma_two = 1.0 / (2.0 / sigma_one - sigma_one)
    live = (
        (lax.broadcasted_iota(jnp.int32, (blocks, tile_size), 1) < row_counts[:, None])
        .astype(jnp.float32)
        .reshape(rows_dev)
    )
    extra_rows = tile_rows[blocks:]
    onehot = (extra_rows[:, None] == lax.broadcasted_iota(jnp.int32, (1, blocks), 1)).astype(
        jnp.float32
    )
    col_index = tile_cols + HB

    def apply_tiles(source):
        extended = with_halo(source, (("slab", 1),), HB * tile_size)
        col_blocks = extended.reshape(norb_dev, blocks + 2 * HB, tile_size)
        picked = jnp.take(col_blocks, col_index, axis=1)
        products = jnp.einsum("otc,trc->otr", picked, tiles, preferred_element_type=jnp.float32)
        diagonal_part = products[:, :blocks]
        extra_part = jnp.einsum(
            "otr,tb->obr", products[:, blocks:], onehot, precision=lax.Precision.HIGH
        )
        summed = diagonal_part + extra_part
        return summed.reshape(norb_dev, rows_dev)

    source = orbitals_t.astype(jnp.float32)
    applied = apply_tiles(orbitals_t)
    filtered_one = (live * (applied - center * source) * (sigma_one / half_width)).astype(
        jnp.bfloat16
    )
    applied = apply_tiles(filtered_one)
    first = filtered_one.astype(jnp.float32)
    filtered_two = (
        live
        * (
            (applied - center * first) * (2.0 * sigma_two / half_width)
            - sigma_one * sigma_two * source
        )
    ).astype(jnp.bfloat16)
    row_major = lax.all_to_all(filtered_two, "orb", split_axis=1, concat_axis=0, tiled=True)
    rotated = jnp.einsum(
        "kj,kr->jr",
        lax.all_gather(rotation, "orb", axis=0, tiled=True),
        row_major,
        preferred_element_type=jnp.float32,
    ).astype(jnp.bfloat16)
    return lax.all_to_all(rotated, "orb", split_axis=0, concat_axis=1, tiled=True)


def local(orbitals_t, tiles, *rest):
    slabs, orbs = lax.axis_size("slab"), lax.axis_size("orb")
    fits = slabs == 2 and orbs == PLANE * PLANE and orbitals_t.shape[0] % tiles.shape[1] == 0
    return (paired if fits else general)(orbitals_t, tiles, *rest)


def solution(mesh):
    return jax.shard_map(
        local,
        mesh=mesh,
        in_specs=(
            P("orb", "slab"),
            P("slab", None, None),
            P("slab"),
            P("slab"),
            P("slab"),
            P(),
            P("orb", None),
        ),
        out_specs=P("orb", "slab"),
        check_vma=False,
    )
```

```python
import functools

import jax
import jax.numpy as jnp
from jax import lax
from jax.experimental import pallas as pl
from jax.experimental.pallas import tpu as pltpu
from jax.sharding import PartitionSpec as P

HB = 2
EDGE = 2 * HB
GROUP = 8
PLANE = 4
ORDER = (0, 2, 3, 1)
VMEM = pl.BlockSpec(memory_space=pltpu.VMEM)
HBM = pl.BlockSpec(memory_space=pltpu.HBM)
SMEM = pl.BlockSpec(memory_space=pltpu.SMEM)
MIB = 1024 * 1024
f32, bf16 = jnp.float32, jnp.bfloat16


def call(body, limit, out_shape, in_specs, scratch_shapes=(), moved=1000, out_specs=None, **options):
    return pl.pallas_call(
        body,
        out_shape=out_shape,
        in_specs=in_specs,
        out_specs=out_specs or jax.tree.map(lambda _: VMEM, out_shape),
        scratch_shapes=scratch_shapes,
        compiler_params=pltpu.CompilerParams(vmem_limit_bytes=limit * MIB),
        cost_estimate=pl.CostEstimate(flops=1000, bytes_accessed=moved, transcendentals=0),
        **options,
    )


def after(value, *done):
    return lax.optimization_barrier((value, done))[0]


def coefficients(bounds_ref):
    lower_bound = -3.0 + bounds_ref[0]
    cutoff = bounds_ref[1] - 0.5
    upper_bound = 3.0 + bounds_ref[2]
    half_width = (upper_bound - cutoff) / 2.0
    center = (upper_bound + cutoff) / 2.0
    sigma_one = half_width / (lower_bound - center)
    sigma_two = 1.0 / (2.0 / sigma_one - sigma_one)
    return center, sigma_one / half_width, 2.0 * sigma_two / half_width, sigma_one * sigma_two


def loop(start, stop, body, unroll, carry=0):
    return lax.fori_loop(start, stop, body, carry, unroll=unroll)


def product(tile, block):
    return jnp.dot(tile, block, preferred_element_type=f32)


def is_edge(row, blocks):
    return (row < HB) | (row >= blocks - HB)


def edge_slot(row, blocks):
    return jnp.where(row < HB, row, row - blocks + EDGE)


def edge_row(slot, blocks):
    return slot if slot < HB else blocks - EDGE + slot


def live_mask(tile, lanes, count):
    return lax.broadcasted_iota(jnp.int32, (tile, lanes), 0) < count


def sum_counts(counts_ref, rows):
    total = 0
    for r in rows:
        total = total + counts_ref[r]
    return total


def start_kernel(groups, place_ref, x_ref, rotation_ref, halo_ref, xt_ref, *refs):
    pieces, sems = refs[:-1], refs[-1]
    width = halo_ref.shape[1]
    z, slab, p = place_ref[0], place_ref[1], place_ref[2]
    begin = jnp.where(slab == 0, x_ref.shape[1] - width, 0)
    begin = pl.multiple_of(begin, width)
    copies = [pltpu.make_async_copy(x_ref.at[:, pl.ds(begin, width)], halo_ref, sems.at[0])]
    lanes = pieces[0].shape[1] // groups
    half = groups // 2
    for q, ref in enumerate(pieces):
        for h in range(2):
            for g in range(half):
                block = ((slab ^ h) * half + g) * PLANE + (p ^ q)
                begin = pl.multiple_of(block * lanes, lanes)
                at = (h * half + g) * lanes
                copies.append(
                    pltpu.make_async_copy(
                        rotation_ref.at[:, pl.ds(begin, lanes)],
                        ref.at[:, at:at + lanes],
                        sems.at[len(copies)],
                    )
                )
    for copy in copies:
        copy.start()
    blocks, tile = xt_ref.shape[:2]

    def turn(r, _):
        xt_ref[r] = x_ref[:, pl.ds(pl.multiple_of(r * tile, tile), tile)].T
        return 0

    loop(0, blocks, turn, 16)
    for copy in copies:
        copy.wait()


def multiply(blocks, rows_ref, cols_ref, tiles_ref, source_ref, acc_ref, extra_ref):
    def diagonal(r, _):
        acc_ref[r] = product(tiles_ref[r], source_ref[r])
        return 0

    loop(0, blocks, diagonal, 16)
    listed = tiles_ref.shape[0]

    def extra(k, _):
        col = jnp.clip(cols_ref[k], 0, blocks - 1)
        extra_ref[k - blocks] = product(tiles_ref[k], source_ref[col])
        return 0

    loop(blocks, listed, extra, 16)

    def gather(k, _):
        inside = (cols_ref[k] >= 0) & (cols_ref[k] < blocks)
        acc_ref[jnp.where(inside, rows_ref[k], blocks)] += extra_ref[k - blocks]
        return 0

    loop(blocks, listed, gather, 8)


def multiply_edges(blocks, slab, rows_ref, cols_ref, tiles_ref, halo_ref, add):
    def extra(k, _):
        col = cols_ref[k]
        slot = jnp.where(slab == 0, col - blocks, col + HB)

        @pl.when(((col < 0) | (col >= blocks)) & (slot >= 0) & (slot < HB))
        def _():
            add(rows_ref[k], product(tiles_ref[k], halo_ref[slot]))

        return 0

    loop(blocks, tiles_ref.shape[0], extra, 4)


def first_kernel(
    blocks, place_ref, rows_ref, cols_ref, counts_ref, bounds_ref, xt_ref, halo_ref, tiles_ref,
    f1_ref, edge_ref, acc_ref, extra_ref, ext_ref,
):
    tile, lanes = xt_ref.shape[1:]
    slab = place_ref[1]
    multiply(blocks, rows_ref, cols_ref, tiles_ref, xt_ref, acc_ref, extra_ref)
    for b in range(HB):
        ext_ref[b] = halo_ref[:, b * tile:(b + 1) * tile].T

    def add(row, value):
        acc_ref[row] += value

    multiply_edges(blocks, slab, rows_ref, cols_ref, tiles_ref, ext_ref, add)
    center, scale = coefficients(bounds_ref)[:2]

    def finish(r, _):
        value = (acc_ref[r] - center * xt_ref[r].astype(f32)) * scale
        f1_ref[r] = jnp.where(live_mask(tile, lanes, counts_ref[r]), value, 0.0).astype(bf16)
        return 0

    loop(0, blocks, finish, 4)
    begin = jnp.where(slab == 0, blocks - HB, 0)
    for b in range(HB):
        edge_ref[b] = f1_ref[begin + b]


def second_values(r, acc, block, xt_ref, counts_ref, scales):
    tile, lanes = block.shape
    center, _, scale, both = scales
    value = (acc - center * block.astype(f32)) * scale - both * xt_ref[r].astype(f32)
    return jnp.where(live_mask(tile, lanes, counts_ref[r]), value, 0.0)


def split_parts(outs, place_ref, packed_ref, base):
    part = outs[0].shape[0]
    for s, out in zip(ORDER, outs):
        start = pl.multiple_of(base + (place_ref[0] ^ s) * part, 16)
        out[...] = packed_ref[pl.ds(start, part)].astype(bf16)


def second_kernel(
    blocks, groups, place_ref, rows_ref, cols_ref, counts_ref, bounds_ref, f1_ref, xt_ref, tiles_ref,
    *refs,
):
    outs, refs = refs[:groups], refs[groups:]
    shared_ref, excess_ref, rest_ref, edge_ref, acc_ref, extra_ref, packed_ref = refs
    tile = tiles_ref.shape[1]
    multiply(blocks, rows_ref, cols_ref, tiles_ref, f1_ref, acc_ref, extra_ref)
    edges = [edge_row(e, blocks) for e in range(EDGE)]
    for e, r in enumerate(edges):
        edge_ref[e] = acc_ref[r]
    scales = coefficients(bounds_ref)

    def finish(r, offset):
        packed_ref[pl.ds(offset, tile)] = second_values(
            r, acc_ref[r], f1_ref[r], xt_ref, counts_ref, scales
        )
        return offset + counts_ref[r]

    loop(HB, blocks - HB, finish, 4, sum_counts(counts_ref, edges))
    size = rest_ref.shape[0]
    rest_ref[...] = packed_ref[:size]
    split_parts(outs, place_ref, packed_ref, size)
    shared_ref[...] = packed_ref[2 * size:3 * size].astype(bf16)
    excess_ref[...] = packed_ref[3 * size:4 * size].astype(bf16)


def second_edge_kernel(
    blocks, groups, place_ref, rows_ref, cols_ref, counts_ref, bounds_ref, halo_ref, f1_ref, xt_ref,
    tiles_ref, sum_ref, rest_ref, *refs,
):
    outs, (acc_ref, packed_ref) = refs[:groups], refs[groups:]
    tile = tiles_ref.shape[1]
    acc_ref[...] = sum_ref[...]

    def add(row, value):
        acc_ref[edge_slot(row, blocks)] += value

    multiply_edges(blocks, place_ref[1], rows_ref, cols_ref, tiles_ref, halo_ref, add)
    scales = coefficients(bounds_ref)
    packed_ref[...] = rest_ref[...]
    offset = 0
    for e in range(EDGE):
        r = edge_row(e, blocks)
        value = second_values(r, acc_ref[e], f1_ref[r], xt_ref, counts_ref, scales)
        here = pl.ds(offset, tile)
        live = live_mask(tile, value.shape[1], counts_ref[r])
        packed_ref[here] = jnp.where(live, value, packed_ref[here])
        offset = offset + counts_ref[r]
    split_parts(outs, place_ref, packed_ref, 0)


def merge_kernel(blocks, groups, place_ref, counts_ref, shared_ref, excess_ref, *refs):
    outs, packed_ref = refs[:groups], refs[groups]
    size = shared_ref.shape[0]
    live = sum_counts(counts_ref, range(blocks))
    packed_ref[:size] = shared_ref[...].astype(f32)
    packed_ref[pl.ds(jnp.clip(live - 2 * size, 0, size), size)] = excess_ref[...].astype(f32)
    split_parts(outs, place_ref, packed_ref, 0)


def rotate_kernel(
    groups, place_ref, own, over_x, core, mine, near, far_two, far_three, near_more, other_ref, *refs
):
    outs, turned = refs[:groups], refs[groups]
    width = outs[0].shape[1]
    half = groups // 2 * width
    lhs = jnp.concatenate(
        [part for s in range(groups) for part in (own[s], core[0, s], over_x[s], core[1, s])], axis=1
    )

    def wide(ref, at=0):
        rows = mine.shape[0]
        return jnp.concatenate(
            [ref[(at + i) * rows:(at + i + 1) * rows] for i in range(groups // 2)], axis=1
        )

    for h in range(2):
        if h == 0:
            rhs = [far_two[...], wide(far_three), near[...]]
        else:
            rhs = [wide(other_ref), wide(other_ref, groups // 2), wide(near_more)]
        rhs = jnp.concatenate([mine[:, h * half:(h + 1) * half]] + rhs, axis=0)
        total = product(lhs, rhs).astype(bf16)
        first = (place_ref[1] ^ h) * (groups // 2)
        for z in range(groups // 2):
            turned[first + z] = total[:, z * width:(z + 1) * width]
    for s, out in zip(ORDER, outs):
        out[...] = turned[place_ref[0] ^ s]


def spread(blocks, tile, counts_ref, cases, block_ref, out_hbm, sems):
    def copy(b):
        there = out_hbm.at[:, pl.ds(pl.multiple_of(b * tile, tile), tile)]
        return pltpu.make_async_copy(block_ref.at[b], there, sems.at[b])

    def each(act):
        def some(g, offset):
            places = []
            for i in range(g * GROUP, (g + 1) * GROUP):
                b = edge_row(i, blocks) if i < EDGE else i - HB
                places.append((b, offset, offset + counts_ref[b]))
                offset = places[-1][2]
            for wanted, source in cases:
                flags = [wanted(begin, end) for _, begin, end in places]

                @pl.when(functools.reduce(jnp.logical_or, flags))
                def _():
                    act(places, flags, source)

            return offset

        offset = 0
        for g in range(blocks // GROUP):
            offset = some(g, offset)

    def write(places, flags, source):
        for b, begin, _ in places:
            rows = source(begin)
            rows = jnp.where(live_mask(tile, rows.shape[1], counts_ref[b]), rows, 0.0).astype(bf16)
            block_ref[b] = rows.T
        for (b, _, _), flag in zip(places, flags):
            @pl.when(flag)
            def _():
                copy(b).start()

    def wait(places, flags, source):
        for (b, _, _), flag in zip(places, flags):
            @pl.when(flag)
            def _():
                copy(b).wait()

    each(write)
    each(wait)


def spread_kernel(blocks, groups, place_ref, counts_ref, *refs):
    parts, (out_hbm, seam_ref, packed_ref, block_ref, sems) = refs[:-5], refs[-5:]
    part = parts[0].shape[0]
    size = part * groups
    tile = block_ref.shape[1]
    for i in range(2):
        for j, s in enumerate(ORDER):
            start = pl.multiple_of((i * groups + (place_ref[0] ^ s)) * part, 16)
            packed_ref[pl.ds(start, part)] = parts[i * groups + j][...].astype(f32)
    seam_ref[0] = packed_ref[:tile]
    seam_ref[1] = packed_ref[2 * size - tile:2 * size]

    def wanted(begin, end):
        return (begin >= size) & (end <= 3 * size)

    def source(begin):
        return packed_ref[pl.ds(jnp.clip(begin - size, 0, 2 * size), tile)]

    spread(blocks, tile, counts_ref, [(wanted, source)], block_ref, out_hbm, sems)


def spread_rest_kernel(blocks, groups, place_ref, counts_ref, done_hbm, seam_ref, back_ref, *refs):
    parts, (out_hbm, packed_ref, far_ref, block_ref, sems) = refs[:-5], refs[-5:]
    part = parts[0].shape[0]
    size = part * groups
    tile = block_ref.shape[1]
    for j, s in enumerate(ORDER):
        start = pl.multiple_of((place_ref[0] ^ s) * part, 16)
        packed_ref[pl.ds(start, part)] = parts[j][...].astype(f32)
    packed_ref[size:] = seam_ref[0]
    live = sum_counts(counts_ref, range(blocks))

    @pl.when(live > 3 * size)
    def _():
        base = jnp.clip(live - 3 * size, 0, size)
        for j, s in enumerate(ORDER):
            far_ref[pl.ds(base + (place_ref[0] ^ s) * part, part)] = back_ref[
                j * part:(j + 1) * part
            ].astype(f32)

    far_ref[size - tile:size] = seam_ref[1]

    def near(begin, end):
        return begin < size

    def near_source(begin):
        return packed_ref[pl.ds(jnp.minimum(begin, size), tile)]

    def far(begin, end):
        return end > 3 * size

    def far_source(begin):
        return far_ref[pl.ds(jnp.clip(begin - 2 * size, 0, 2 * size), tile)]

    cases = [(near, near_source), (far, far_source)]
    spread(blocks, tile, counts_ref, cases, block_ref, out_hbm, sems)


def paired(orbitals_t, tiles, tile_rows, tile_cols, row_counts, bounds, rotation):
    norb_dev, rows_dev = orbitals_t.shape
    listed, tile = tiles.shape[:2]
    blocks = rows_dev // tile
    orbs = lax.axis_size("orb")
    groups = orbs // PLANE
    me, slab = lax.axis_index("orb"), lax.axis_index("slab")
    z, p = me // PLANE, me % PLANE
    place = jnp.stack([z, slab, p])
    size = rows_dev // 4
    part = size // groups
    block_shape = (blocks, tile, norb_dev)
    edge_shape = (EDGE, tile, norb_dev)
    halo_shape = (HB, tile, norb_dev)
    extra_shape = (listed - blocks, tile, norb_dev)
    size_shape = (size, norb_dev)
    lists = (place, tile_rows, tile_cols, row_counts, bounds)

    def shaped(shape, dtype=bf16):
        return jax.ShapeDtypeStruct(shape, dtype)

    part_outs = [shaped((part, norb_dev))] * groups

    def swap(value, bits):
        return lax.ppermute(value, "orb", [(i, i ^ bits) for i in range(orbs)])

    def over_z(values):
        return [swap(v, s * PLANE) if s else v for s, v in zip(ORDER, values)]

    def other_slab(value):
        return lax.ppermute(value, "slab", [(0, 1), (1, 0)])

    half = groups // 2 * norb_dev
    halo, xt, *pieces = call(
        functools.partial(start_kernel, groups),
        20,
        [shaped((norb_dev, HB * tile)), shaped(block_shape)]
        + [shaped((norb_dev, 2 * half))] * PLANE,
        [SMEM, VMEM, HBM],
        [pltpu.SemaphoreType.DMA((1 + PLANE * groups,))],
        moved=20 * MIB,
    )(place, orbitals_t, rotation)
    halo = other_slab(halo)
    mine = [pieces[0]] + [swap(pieces[q], q) for q in range(1, PLANE)]
    mine = jnp.concatenate(after(mine, halo), axis=0)
    far_two = swap(mine[:, :half], 2 * PLANE)
    near = swap(mine[:, :half], PLANE)
    f1, edge = call(
        functools.partial(first_kernel, blocks),
        16,
        [shaped(block_shape), shaped(halo_shape)],
        [SMEM] * 5 + [VMEM] * 3,
        [
            pltpu.VMEM((blocks + 1, tile, norb_dev), f32),
            pltpu.VMEM(extra_shape, f32),
            pltpu.VMEM(halo_shape, bf16),
        ],
    )(*lists, xt, halo, tiles)
    halo = other_slab(edge)

    *first_parts, shared, excess, rest, edge_sum = call(
        functools.partial(second_kernel, blocks, groups),
        18,
        part_outs
        + [shaped(size_shape)] * 2 + [shaped(size_shape, f32), shaped(edge_shape, f32)],
        [SMEM] * 5 + [VMEM] * 3,
        [
            pltpu.VMEM((blocks + 1, tile, norb_dev), f32),
            pltpu.VMEM(extra_shape, f32),
            pltpu.VMEM((rows_dev + tile, norb_dev), f32),
        ],
    )(*lists, f1, xt, tiles)

    def together(*values):
        return lax.optimization_barrier(values)

    def over_core(own, over_x):
        return swap(jnp.stack([own, over_x]), 1)

    def rotate(*gathered):
        return call(
            functools.partial(rotate_kernel, groups),
            12,
            part_outs,
            [SMEM] + [VMEM] * (3 + len(weights)),
            [pltpu.VMEM((groups, part, norb_dev), bf16)],
        )(place, *gathered, *weights)

    excess, halo, first_parts, near, far_two = together(excess, halo, first_parts, near, far_two)
    excess = other_slab(excess)
    columns = [far_two[:, i * norb_dev:(i + 1) * norb_dev] for i in range(groups // 2)]
    first = over_z([*first_parts[:3], jnp.concatenate([first_parts[3]] + columns)])
    shared_parts = call(
        functools.partial(merge_kernel, blocks, groups),
        8,
        part_outs,
        [SMEM] * 2 + [VMEM] * 2,
        [pltpu.VMEM((2 * size, norb_dev), f32)],
    )(place, row_counts, shared, excess)

    first, shared_parts, rest = together(first, shared_parts, rest)
    far_three, first[3] = first[3][part:], first[3][:part]
    columns_near = [mine[:, half + i * norb_dev:half + (i + 1) * norb_dev] for i in range(groups // 2)]
    shared = over_z([*shared_parts[:3], jnp.concatenate([shared_parts[3]] + columns_near)])
    first_own = jnp.stack(first)
    first_x = swap(first_own, 2)
    others = other_slab(jnp.concatenate(columns + [far_three]))
    rest_parts = call(
        functools.partial(second_edge_kernel, blocks, groups),
        8,
        part_outs,
        [SMEM] * 5 + [VMEM] * 6,
        [pltpu.VMEM(edge_shape, f32), pltpu.VMEM(size_shape, f32)],
    )(*lists, halo, f1, xt, tiles, edge_sum, rest)

    shared, first_x, rest_parts, others = together(shared, first_x, rest_parts, others)
    near_more, shared[3] = shared[3][part:], shared[3][:part]
    rest = over_z(rest_parts)
    first_core = over_core(first_own, first_x)
    shared_own = jnp.stack(shared)
    shared_x = swap(shared_own, 2)
    weights = [mine, near, far_two, far_three, near_more, others]
    first_turned = rotate(first_own, first_x, first_core)

    rest, first_turned, shared_x = together(rest, first_turned, shared_x)
    first_back = over_z(first_turned)
    shared_core = over_core(shared_own, shared_x)
    rest_own = jnp.stack(rest)
    rest_x = swap(rest_own, 2)
    shared_turned = rotate(shared_own, shared_x, shared_core)

    first_back, shared_turned, rest_x = together(first_back, shared_turned, rest_x)
    shared_back = over_z(shared_turned)
    rest_core = over_core(rest_own, rest_x)
    rest_turned = rotate(rest_own, rest_x, rest_core)

    shared_back, rest_turned = together(shared_back, rest_turned)
    rest_back = over_z(rest_turned)
    back = other_slab(jnp.concatenate(shared_back))
    width_shape = (blocks, norb_dev, tile)
    out = shaped((norb_dev, rows_dev))
    done, seam = call(
        functools.partial(spread_kernel, blocks, groups),
        12,
        [out, shaped((2, tile, norb_dev), f32)],
        [SMEM] * 2 + [VMEM] * (2 * groups),
        [
            pltpu.VMEM((2 * size + tile, norb_dev), f32),
            pltpu.VMEM(width_shape, bf16),
            pltpu.SemaphoreType.DMA((blocks,)),
        ],
        out_specs=[HBM, VMEM],
    )(place, row_counts, *first_back, *shared_back)
    return call(
        functools.partial(spread_rest_kernel, blocks, groups),
        12,
        out,
        [SMEM] * 2 + [HBM] + [VMEM] * (2 + groups),
        [
            pltpu.VMEM((size + tile, norb_dev), f32),
            pltpu.VMEM((2 * size + tile, norb_dev), f32),
            pltpu.VMEM(width_shape, bf16),
            pltpu.SemaphoreType.DMA((blocks,)),
        ],
        out_specs=HBM,
        input_output_aliases={2: 0},
    )(place, row_counts, done, seam, back, *rest_back)


def with_halo(block, sides, width):
    for axis, dim in sides:
        count = lax.axis_size(axis)
        forward = [(i, i + 1) for i in range(count - 1)]
        backward = [(target, source) for source, target in forward]
        low = lax.ppermute(
            lax.slice_in_dim(block, block.shape[dim] - width, None, axis=dim), axis, forward
        )
        high = lax.ppermute(lax.slice_in_dim(block, 0, width, axis=dim), axis, backward)
        block = jnp.concatenate([low, block, high], axis=dim)
    return block


def general(orbitals_t, tiles, tile_rows, tile_cols, row_counts, bounds, rotation):
    norb_dev, rows_dev = orbitals_t.shape
    tile_size = tiles.shape[1]
    blocks = rows_dev // tile_size
    lower_bound = -3.0 + bounds[0]
    cutoff = bounds[1] - 0.5
    upper_bound = 3.0 + bounds[2]
    half_width = (upper_bound - cutoff) / 2.0
    center = (upper_bound + cutoff) / 2.0
    sigma_one = half_width / (lower_bound - center)
    sigma_two = 1.0 / (2.0 / sigma_one - sigma_one)
    live = (
        (lax.broadcasted_iota(jnp.int32, (blocks, tile_size), 1) < row_counts[:, None])
        .astype(jnp.float32)
        .reshape(rows_dev)
    )
    extra_rows = tile_rows[blocks:]
    onehot = (extra_rows[:, None] == lax.broadcasted_iota(jnp.int32, (1, blocks), 1)).astype(
        jnp.float32
    )
    col_index = tile_cols + HB

    def apply_tiles(source):
        extended = with_halo(source, (("slab", 1),), HB * tile_size)
        col_blocks = extended.reshape(norb_dev, blocks + 2 * HB, tile_size)
        picked = jnp.take(col_blocks, col_index, axis=1)
        products = jnp.einsum("otc,trc->otr", picked, tiles, preferred_element_type=jnp.float32)
        diagonal_part = products[:, :blocks]
        extra_part = jnp.einsum(
            "otr,tb->obr", products[:, blocks:], onehot, precision=lax.Precision.HIGH
        )
        summed = diagonal_part + extra_part
        return summed.reshape(norb_dev, rows_dev)

    source = orbitals_t.astype(jnp.float32)
    applied = apply_tiles(orbitals_t)
    filtered_one = (live * (applied - center * source) * (sigma_one / half_width)).astype(
        jnp.bfloat16
    )
    applied = apply_tiles(filtered_one)
    first = filtered_one.astype(jnp.float32)
    filtered_two = (
        live
        * (
            (applied - center * first) * (2.0 * sigma_two / half_width)
            - sigma_one * sigma_two * source
        )
    ).astype(jnp.bfloat16)
    row_major = lax.all_to_all(filtered_two, "orb", split_axis=1, concat_axis=0, tiled=True)
    rotated = jnp.einsum(
        "kj,kr->jr",
        lax.all_gather(rotation, "orb", axis=0, tiled=True),
        row_major,
        preferred_element_type=jnp.float32,
    ).astype(jnp.bfloat16)
    return lax.all_to_all(rotated, "orb", split_axis=0, concat_axis=1, tiled=True)


def local(orbitals_t, tiles, *rest):
    slabs, orbs = lax.axis_size("slab"), lax.axis_size("orb")
    fits = slabs == 2 and orbs == PLANE * PLANE and orbitals_t.shape[0] % tiles.shape[1] == 0
    return (paired if fits else general)(orbitals_t, tiles, *rest)


def solution(mesh):
    return jax.shard_map(
        local,
        mesh=mesh,
        in_specs=(
            P("orb", "slab"),
            P("slab", None, None),
            P("slab"),
            P("slab"),
            P("slab"),
            P(),
            P("orb", None),
        ),
        out_specs=P("orb", "slab"),
        check_vma=False,
    )
```

```python
import functools

import jax
import jax.numpy as jnp
from jax import lax
from jax.experimental import pallas as pl
from jax.experimental.pallas import tpu as pltpu
from jax.sharding import PartitionSpec as P

HB = 2
EDGE = 2 * HB
GROUP = 8
PLANE = 4
ORDER = (0, 3, 2, 1)
VMEM = pl.BlockSpec(memory_space=pltpu.VMEM)
HBM = pl.BlockSpec(memory_space=pltpu.HBM)
SMEM = pl.BlockSpec(memory_space=pltpu.SMEM)
MIB = 1024 * 1024
f32, bf16 = jnp.float32, jnp.bfloat16


def call(body, limit, out_shape, in_specs, scratch_shapes=(), moved=1000, out_specs=None, **options):
    return pl.pallas_call(
        body,
        out_shape=out_shape,
        in_specs=in_specs,
        out_specs=out_specs or jax.tree.map(lambda _: VMEM, out_shape),
        scratch_shapes=scratch_shapes,
        compiler_params=pltpu.CompilerParams(vmem_limit_bytes=limit * MIB),
        cost_estimate=pl.CostEstimate(flops=1000, bytes_accessed=moved, transcendentals=0),
        **options,
    )


def after(value, *done):
    return lax.optimization_barrier((value, done))[0]


def coefficients(bounds_ref):
    lower_bound = -3.0 + bounds_ref[0]
    cutoff = bounds_ref[1] - 0.5
    upper_bound = 3.0 + bounds_ref[2]
    half_width = (upper_bound - cutoff) / 2.0
    center = (upper_bound + cutoff) / 2.0
    sigma_one = half_width / (lower_bound - center)
    sigma_two = 1.0 / (2.0 / sigma_one - sigma_one)
    first, second, last = sigma_one / half_width, 2.0 * sigma_two / half_width, sigma_one * half_width / 2.0
    return center, first, second, last


def loop(start, stop, body, unroll, carry=0):
    return lax.fori_loop(start, stop, body, carry, unroll=unroll)


def product(tile, block):
    return jnp.dot(tile, block, preferred_element_type=f32)


def is_edge(row, blocks):
    return (row < HB) | (row >= blocks - HB)


def edge_slot(row, blocks):
    return jnp.where(row < HB, row, row - blocks + EDGE)


def edge_row(slot, blocks):
    return slot if slot < HB else blocks - EDGE + slot


def live_mask(tile, lanes, count):
    return lax.broadcasted_iota(jnp.int32, (tile, lanes), 0) < count


def sum_counts(counts_ref, rows):
    total = 0
    for r in rows:
        total = total + counts_ref[r]
    return total


def start_kernel(groups, place_ref, x_ref, rotation_ref, halo_ref, xt_ref, *refs):
    pieces, sems = refs[:-1], refs[-1]
    width = halo_ref.shape[1]
    z, slab, p = place_ref[0], place_ref[1], place_ref[2]
    begin = jnp.where(slab == 0, x_ref.shape[1] - width, 0)
    begin = pl.multiple_of(begin, width)
    copies = [pltpu.make_async_copy(x_ref.at[:, pl.ds(begin, width)], halo_ref, sems.at[0])]
    lanes = pieces[0].shape[1] // groups
    half = groups // 2
    for q, ref in enumerate(pieces):
        for h in range(2):
            for g in range(half):
                block = ((slab ^ h) * half + g) * PLANE + (p ^ q)
                begin = pl.multiple_of(block * lanes, lanes)
                at = (h * half + g) * lanes
                copies.append(
                    pltpu.make_async_copy(
                        rotation_ref.at[:, pl.ds(begin, lanes)],
                        ref.at[:, at:at + lanes],
                        sems.at[len(copies)],
                    )
                )
    for copy in copies:
        copy.start()
    blocks, tile = xt_ref.shape[:2]

    def turn(r, _):
        xt_ref[r] = x_ref[:, pl.ds(pl.multiple_of(r * tile, tile), tile)].T
        return 0

    loop(0, blocks, turn, 16)
    for copy in copies:
        copy.wait()


def multiply(blocks, rows_ref, cols_ref, tiles_ref, source_ref, acc_ref, extra_ref, more):
    def diagonal(r, _):
        acc_ref[r] = product(tiles_ref[r], source_ref[r]) - more(r)
        return 0

    loop(0, blocks, diagonal, 16)
    listed = tiles_ref.shape[0]

    def extra(k, _):
        col = jnp.clip(cols_ref[k], 0, blocks - 1)
        extra_ref[k - blocks] = product(tiles_ref[k], source_ref[col])
        return 0

    loop(blocks, listed, extra, 16)

    def gather(k, _):
        inside = (cols_ref[k] >= 0) & (cols_ref[k] < blocks)
        acc_ref[jnp.where(inside, rows_ref[k], blocks)] += extra_ref[k - blocks]
        return 0

    loop(blocks, listed, gather, 8)


def multiply_edges(blocks, slab, rows_ref, cols_ref, tiles_ref, halo_ref, add):
    def extra(k, _):
        col = cols_ref[k]
        slot = jnp.where(slab == 0, col - blocks, col + HB)

        @pl.when(((col < 0) | (col >= blocks)) & (slot >= 0) & (slot < HB))
        def _():
            add(rows_ref[k], product(tiles_ref[k], halo_ref[slot]))

        return 0

    loop(blocks, tiles_ref.shape[0], extra, 4)


def first_kernel(
    blocks, place_ref, rows_ref, cols_ref, counts_ref, bounds_ref, xt_ref, halo_ref, tiles_ref,
    f1_ref, edge_ref, acc_ref, extra_ref, ext_ref,
):
    tile, lanes = xt_ref.shape[1:]
    slab = place_ref[1]
    center, scale = coefficients(bounds_ref)[:2]

    def more(r):
        return center * xt_ref[r].astype(f32)

    multiply(blocks, rows_ref, cols_ref, tiles_ref, xt_ref, acc_ref, extra_ref, more)
    for b in range(HB):
        ext_ref[b] = halo_ref[:, b * tile:(b + 1) * tile].T

    def add(row, value):
        acc_ref[row] += value

    multiply_edges(blocks, slab, rows_ref, cols_ref, tiles_ref, ext_ref, add)
    def finish(r, _):
        live = live_mask(tile, lanes, counts_ref[r])
        f1_ref[r] = jnp.where(live, acc_ref[r] * scale, 0.0).astype(bf16)
        return 0

    loop(0, blocks, finish, 4)
    begin = jnp.where(slab == 0, blocks - HB, 0)
    for b in range(HB):
        edge_ref[b] = f1_ref[begin + b]


def split_parts(outs, place_ref, packed_ref, base):
    part = outs[0].shape[0]
    for s, out in zip(ORDER, outs):
        start = pl.multiple_of(base + (place_ref[0] ^ s) * part, 16)
        out[...] = packed_ref[pl.ds(start, part)].astype(bf16)


def second_kernel(
    blocks, groups, place_ref, rows_ref, cols_ref, counts_ref, bounds_ref, f1_ref, xt_ref, tiles_ref,
    *refs,
):
    outs, refs = refs[:groups], refs[groups:]
    shared_ref, excess_ref, rest_ref, edge_ref, acc_ref, extra_ref, packed_ref = refs
    tile = tiles_ref.shape[1]
    center, _, scale, last = coefficients(bounds_ref)

    def more(r):
        return center * f1_ref[r].astype(f32) + last * xt_ref[r].astype(f32)

    multiply(blocks, rows_ref, cols_ref, tiles_ref, f1_ref, acc_ref, extra_ref, more)
    edges = [edge_row(e, blocks) for e in range(EDGE)]
    for e, r in enumerate(edges):
        edge_ref[e] = acc_ref[r]
    def finish(r, offset):
        live = live_mask(tile, acc_ref.shape[2], counts_ref[r])
        packed_ref[pl.ds(offset, tile)] = jnp.where(live, acc_ref[r] * scale, 0.0)
        return offset + counts_ref[r]

    loop(HB, blocks - HB, finish, 4, sum_counts(counts_ref, edges))
    size = rest_ref.shape[0]
    rest_ref[...] = packed_ref[:size]
    split_parts(outs, place_ref, packed_ref, size)
    shared_ref[...] = packed_ref[2 * size:3 * size].astype(bf16)
    excess_ref[...] = packed_ref[3 * size:4 * size].astype(bf16)


def second_edge_kernel(
    blocks, groups, place_ref, rows_ref, cols_ref, counts_ref, bounds_ref, halo_ref, tiles_ref,
    sum_ref, rest_ref, *refs,
):
    outs, (acc_ref, packed_ref) = refs[:groups], refs[groups:]
    tile = tiles_ref.shape[1]
    acc_ref[...] = sum_ref[...]

    def add(row, value):
        acc_ref[edge_slot(row, blocks)] += value

    multiply_edges(blocks, place_ref[1], rows_ref, cols_ref, tiles_ref, halo_ref, add)
    scale = coefficients(bounds_ref)[2]
    packed_ref[...] = rest_ref[...]
    offset = 0
    for e in range(EDGE):
        r = edge_row(e, blocks)
        here = pl.ds(offset, tile)
        live = live_mask(tile, acc_ref.shape[2], counts_ref[r])
        packed_ref[here] = jnp.where(live, acc_ref[e] * scale, packed_ref[here])
        offset = offset + counts_ref[r]
    split_parts(outs, place_ref, packed_ref, 0)


def merge_kernel(blocks, groups, place_ref, counts_ref, shared_ref, excess_ref, *refs):
    outs, packed_ref = refs[:groups], refs[groups]
    size = shared_ref.shape[0]
    live = sum_counts(counts_ref, range(blocks))
    packed_ref[:size] = shared_ref[...].astype(f32)
    packed_ref[pl.ds(jnp.clip(live - 2 * size, 0, size), size)] = excess_ref[...].astype(f32)
    split_parts(outs, place_ref, packed_ref, 0)


def rotate_kernel(
    groups, place_ref, own, over_x, core, mine, near, far_two, far_three, other_near, other_ref, *refs
):
    outs, turned = refs[:groups], refs[groups]
    width = outs[0].shape[1]
    half = groups // 2 * width
    lhs = jnp.concatenate(
        [part for s in range(groups) for part in (own[s], core[0, s], over_x[s], core[1, s])], axis=1
    )

    def wide(ref, at=0):
        rows = mine.shape[0]
        return jnp.concatenate(
            [ref[(at + i) * rows:(at + i + 1) * rows] for i in range(groups // 2)], axis=1
        )

    for h in range(2):
        own_half = mine[:, h * half:(h + 1) * half]
        if h == 0:
            rhs = [own_half, near[...], far_two[...], wide(far_three)]
        else:
            rhs = [own_half, other_near[...], wide(other_ref), wide(other_ref, groups // 2)]
        rhs = jnp.concatenate([rhs[s] for s in ORDER], axis=0)
        total = product(lhs, rhs).astype(bf16)
        first = (place_ref[1] ^ h) * (groups // 2)
        for z in range(groups // 2):
            turned[first + z] = total[:, z * width:(z + 1) * width]
    for s, out in zip(ORDER, outs):
        out[...] = turned[place_ref[0] ^ s]


def spread(blocks, tile, counts_ref, cases, block_ref, out_hbm, sems):
    def copy(b):
        there = out_hbm.at[:, pl.ds(pl.multiple_of(b * tile, tile), tile)]
        return pltpu.make_async_copy(block_ref.at[b], there, sems.at[b])

    def each(act):
        def some(g, offset):
            places = []
            for i in range(g * GROUP, (g + 1) * GROUP):
                b = edge_row(i, blocks) if i < EDGE else i - HB
                places.append((b, offset, offset + counts_ref[b]))
                offset = places[-1][2]
            for wanted, source in cases:
                flags = [wanted(begin, end) for _, begin, end in places]

                @pl.when(functools.reduce(jnp.logical_or, flags))
                def _():
                    act(places, flags, source)

            return offset

        offset = 0
        for g in range(blocks // GROUP):
            offset = some(g, offset)

    def write(places, flags, source):
        for b, begin, _ in places:
            rows = source(begin)
            rows = jnp.where(live_mask(tile, rows.shape[1], counts_ref[b]), rows, 0.0).astype(bf16)
            block_ref[b] = rows.T
        for (b, _, _), flag in zip(places, flags):
            @pl.when(flag)
            def _():
                copy(b).start()

    def wait(places, flags, source):
        for (b, _, _), flag in zip(places, flags):
            @pl.when(flag)
            def _():
                copy(b).wait()

    each(write)
    each(wait)


def spread_kernel(blocks, groups, place_ref, counts_ref, *refs):
    parts, (out_hbm, seam_ref, packed_ref, block_ref, sems) = refs[:-5], refs[-5:]
    part = parts[0].shape[0]
    size = part * groups
    tile = block_ref.shape[1]
    for i in range(2):
        for j, s in enumerate(ORDER):
            start = pl.multiple_of((i * groups + (place_ref[0] ^ s)) * part, 16)
            packed_ref[pl.ds(start, part)] = parts[i * groups + j][...].astype(f32)
    seam_ref[0] = packed_ref[:tile]
    seam_ref[1] = packed_ref[2 * size - tile:2 * size]

    def wanted(begin, end):
        return (begin >= size) & (end <= 3 * size)

    def source(begin):
        return packed_ref[pl.ds(jnp.clip(begin - size, 0, 2 * size), tile)]

    spread(blocks, tile, counts_ref, [(wanted, source)], block_ref, out_hbm, sems)


def spread_rest_kernel(blocks, groups, place_ref, counts_ref, done_hbm, seam_ref, back_ref, *refs):
    parts, (out_hbm, packed_ref, far_ref, block_ref, sems) = refs[:-5], refs[-5:]
    part = parts[0].shape[0]
    size = part * groups
    tile = block_ref.shape[1]
    for j, s in enumerate(ORDER):
        start = pl.multiple_of((place_ref[0] ^ s) * part, 16)
        packed_ref[pl.ds(start, part)] = parts[j][...].astype(f32)
    packed_ref[size:] = seam_ref[0]
    live = sum_counts(counts_ref, range(blocks))

    @pl.when(live > 3 * size)
    def _():
        base = jnp.clip(live - 3 * size, 0, size)
        for j, s in enumerate(ORDER):
            far_ref[pl.ds(base + (place_ref[0] ^ s) * part, part)] = back_ref[
                j * part:(j + 1) * part
            ].astype(f32)

    far_ref[size - tile:size] = seam_ref[1]

    def near(begin, end):
        return begin < size

    def near_source(begin):
        return packed_ref[pl.ds(jnp.minimum(begin, size), tile)]

    def far(begin, end):
        return end > 3 * size

    def far_source(begin):
        return far_ref[pl.ds(jnp.clip(begin - 2 * size, 0, 2 * size), tile)]

    cases = [(near, near_source), (far, far_source)]
    spread(blocks, tile, counts_ref, cases, block_ref, out_hbm, sems)


def paired(orbitals_t, tiles, tile_rows, tile_cols, row_counts, bounds, rotation):
    norb_dev, rows_dev = orbitals_t.shape
    listed, tile = tiles.shape[:2]
    blocks = rows_dev // tile
    orbs = lax.axis_size("orb")
    groups = orbs // PLANE
    me, slab = lax.axis_index("orb"), lax.axis_index("slab")
    z, p = me // PLANE, me % PLANE
    place = jnp.stack([z, slab, p])
    size = rows_dev // 4
    part = size // groups
    block_shape = (blocks, tile, norb_dev)
    edge_shape = (EDGE, tile, norb_dev)
    halo_shape = (HB, tile, norb_dev)
    extra_shape = (listed - blocks, tile, norb_dev)
    size_shape = (size, norb_dev)
    lists = (place, tile_rows, tile_cols, row_counts, bounds)

    def shaped(shape, dtype=bf16):
        return jax.ShapeDtypeStruct(shape, dtype)

    part_outs = [shaped((part, norb_dev))] * groups

    def swap(value, bits):
        return lax.ppermute(value, "orb", [(i, i ^ bits) for i in range(orbs)])

    def over_z(values):
        return [swap(v, s * PLANE) if s else v for s, v in zip(ORDER, values)]

    def other_slab(value):
        return lax.ppermute(value, "slab", [(0, 1), (1, 0)])

    half = groups // 2 * norb_dev
    halo, xt, *pieces = call(
        functools.partial(start_kernel, groups),
        20,
        [shaped((norb_dev, HB * tile)), shaped(block_shape)]
        + [shaped((norb_dev, 2 * half))] * PLANE,
        [SMEM, VMEM, HBM],
        [pltpu.SemaphoreType.DMA((1 + PLANE * groups,))],
        moved=20 * MIB,
    )(place, orbitals_t, rotation)
    halo = other_slab(halo)
    mine = [pieces[0]] + [swap(pieces[q], q) for q in range(1, PLANE)]
    mine = jnp.concatenate(after(mine, halo), axis=0)
    far_two = swap(mine[:, :half], 2 * PLANE)
    near = swap(mine[:, :half], PLANE)
    f1, edge = call(
        functools.partial(first_kernel, blocks),
        16,
        [shaped(block_shape), shaped(halo_shape)],
        [SMEM] * 5 + [VMEM] * 3,
        [
            pltpu.VMEM((blocks + 1, tile, norb_dev), f32),
            pltpu.VMEM(extra_shape, f32),
            pltpu.VMEM(halo_shape, bf16),
        ],
    )(*lists, xt, halo, tiles)
    halo = other_slab(edge)

    *first_parts, shared, excess, rest, edge_sum = call(
        functools.partial(second_kernel, blocks, groups),
        18,
        part_outs
        + [shaped(size_shape)] * 2 + [shaped(size_shape, f32), shaped(edge_shape, f32)],
        [SMEM] * 5 + [VMEM] * 3,
        [
            pltpu.VMEM((blocks + 1, tile, norb_dev), f32),
            pltpu.VMEM(extra_shape, f32),
            pltpu.VMEM((rows_dev + tile, norb_dev), f32),
        ],
    )(*lists, f1, xt, tiles)

    def together(*values):
        return lax.optimization_barrier(values)

    def over_core(own, over_x):
        return swap(jnp.stack([own, over_x]), 1)

    def rotate(*gathered):
        return call(
            functools.partial(rotate_kernel, groups),
            12,
            part_outs,
            [SMEM] + [VMEM] * (3 + len(weights)),
            [pltpu.VMEM((groups, part, norb_dev), bf16)],
        )(place, *gathered, *weights)

    excess, halo, first_parts, near, far_two = together(excess, halo, first_parts, near, far_two)
    excess = other_slab(excess)
    other_near = other_slab(near)
    columns = [far_two[:, i * norb_dev:(i + 1) * norb_dev] for i in range(groups // 2)]
    first_parts = list(first_parts)
    nearest = ORDER.index(1)
    first_parts[nearest] = jnp.concatenate([first_parts[nearest]] + columns)
    first = over_z(first_parts)
    shared_parts = call(
        functools.partial(merge_kernel, blocks, groups),
        8,
        part_outs,
        [SMEM] * 2 + [VMEM] * 2,
        [pltpu.VMEM((2 * size, norb_dev), f32)],
    )(place, row_counts, shared, excess)

    first, shared_parts, rest, other_near = together(first, shared_parts, rest, other_near)
    far_three, first[nearest] = first[nearest][part:], first[nearest][:part]
    shared = over_z(shared_parts)
    first_own = jnp.stack(first)
    first_x = swap(first_own, 2)
    others = other_slab(jnp.concatenate(columns + [far_three]))
    rest_parts = call(
        functools.partial(second_edge_kernel, blocks, groups),
        8,
        part_outs,
        [SMEM] * 5 + [VMEM] * 4,
        [pltpu.VMEM(edge_shape, f32), pltpu.VMEM(size_shape, f32)],
    )(*lists, halo, tiles, edge_sum, rest)

    shared, first_x, rest_parts, others = together(shared, first_x, rest_parts, others)
    rest = over_z(rest_parts)
    first_core = over_core(first_own, first_x)
    shared_own = jnp.stack(shared)
    shared_x = swap(shared_own, 2)
    weights = [mine, near, far_two, far_three, other_near, others]
    first_turned = rotate(first_own, first_x, first_core)

    rest, first_turned, shared_x = together(rest, first_turned, shared_x)
    first_back = over_z(first_turned)
    shared_core = over_core(shared_own, shared_x)
    rest_own = jnp.stack(rest)
    rest_x = swap(rest_own, 2)
    shared_turned = rotate(shared_own, shared_x, shared_core)

    first_back, shared_turned, rest_x = together(first_back, shared_turned, rest_x)
    shared_back = over_z(shared_turned)
    rest_core = over_core(rest_own, rest_x)
    rest_turned = rotate(rest_own, rest_x, rest_core)

    shared_back, rest_turned = together(shared_back, rest_turned)
    rest_back = over_z(rest_turned)
    back = other_slab(jnp.concatenate(shared_back))
    width_shape = (blocks, norb_dev, tile)
    out = shaped((norb_dev, rows_dev))
    done, seam = call(
        functools.partial(spread_kernel, blocks, groups),
        12,
        [out, shaped((2, tile, norb_dev), f32)],
        [SMEM] * 2 + [VMEM] * (2 * groups),
        [
            pltpu.VMEM((2 * size + tile, norb_dev), f32),
            pltpu.VMEM(width_shape, bf16),
            pltpu.SemaphoreType.DMA((blocks,)),
        ],
        out_specs=[HBM, VMEM],
    )(place, row_counts, *first_back, *shared_back)
    return call(
        functools.partial(spread_rest_kernel, blocks, groups),
        12,
        out,
        [SMEM] * 2 + [HBM] + [VMEM] * (2 + groups),
        [
            pltpu.VMEM((size + tile, norb_dev), f32),
            pltpu.VMEM((2 * size + tile, norb_dev), f32),
            pltpu.VMEM(width_shape, bf16),
            pltpu.SemaphoreType.DMA((blocks,)),
        ],
        out_specs=HBM,
        input_output_aliases={2: 0},
    )(place, row_counts, done, seam, back, *rest_back)


def with_halo(block, sides, width):
    for axis, dim in sides:
        count = lax.axis_size(axis)
        forward = [(i, i + 1) for i in range(count - 1)]
        backward = [(target, source) for source, target in forward]
        low = lax.ppermute(
            lax.slice_in_dim(block, block.shape[dim] - width, None, axis=dim), axis, forward
        )
        high = lax.ppermute(lax.slice_in_dim(block, 0, width, axis=dim), axis, backward)
        block = jnp.concatenate([low, block, high], axis=dim)
    return block


def general(orbitals_t, tiles, tile_rows, tile_cols, row_counts, bounds, rotation):
    norb_dev, rows_dev = orbitals_t.shape
    tile_size = tiles.shape[1]
    blocks = rows_dev // tile_size
    lower_bound = -3.0 + bounds[0]
    cutoff = bounds[1] - 0.5
    upper_bound = 3.0 + bounds[2]
    half_width = (upper_bound - cutoff) / 2.0
    center = (upper_bound + cutoff) / 2.0
    sigma_one = half_width / (lower_bound - center)
    sigma_two = 1.0 / (2.0 / sigma_one - sigma_one)
    live = (
        (lax.broadcasted_iota(jnp.int32, (blocks, tile_size), 1) < row_counts[:, None])
        .astype(jnp.float32)
        .reshape(rows_dev)
    )
    extra_rows = tile_rows[blocks:]
    onehot = (extra_rows[:, None] == lax.broadcasted_iota(jnp.int32, (1, blocks), 1)).astype(
        jnp.float32
    )
    col_index = tile_cols + HB

    def apply_tiles(source):
        extended = with_halo(source, (("slab", 1),), HB * tile_size)
        col_blocks = extended.reshape(norb_dev, blocks + 2 * HB, tile_size)
        picked = jnp.take(col_blocks, col_index, axis=1)
        products = jnp.einsum("otc,trc->otr", picked, tiles, preferred_element_type=jnp.float32)
        diagonal_part = products[:, :blocks]
        extra_part = jnp.einsum(
            "otr,tb->obr", products[:, blocks:], onehot, precision=lax.Precision.HIGH
        )
        summed = diagonal_part + extra_part
        return summed.reshape(norb_dev, rows_dev)

    source = orbitals_t.astype(jnp.float32)
    applied = apply_tiles(orbitals_t)
    filtered_one = (live * (applied - center * source) * (sigma_one / half_width)).astype(
        jnp.bfloat16
    )
    applied = apply_tiles(filtered_one)
    first = filtered_one.astype(jnp.float32)
    filtered_two = (
        live
        * (
            (applied - center * first) * (2.0 * sigma_two / half_width)
            - sigma_one * sigma_two * source
        )
    ).astype(jnp.bfloat16)
    row_major = lax.all_to_all(filtered_two, "orb", split_axis=1, concat_axis=0, tiled=True)
    rotated = jnp.einsum(
        "kj,kr->jr",
        lax.all_gather(rotation, "orb", axis=0, tiled=True),
        row_major,
        preferred_element_type=jnp.float32,
    ).astype(jnp.bfloat16)
    return lax.all_to_all(rotated, "orb", split_axis=0, concat_axis=1, tiled=True)


def local(orbitals_t, tiles, *rest):
    slabs, orbs = lax.axis_size("slab"), lax.axis_size("orb")
    fits = slabs == 2 and orbs == PLANE * PLANE and orbitals_t.shape[0] % tiles.shape[1] == 0
    return (paired if fits else general)(orbitals_t, tiles, *rest)


def solution(mesh):
    return jax.shard_map(
        local,
        mesh=mesh,
        in_specs=(
            P("orb", "slab"),
            P("slab", None, None),
            P("slab"),
            P("slab"),
            P("slab"),
            P(),
            P("orb", None),
        ),
        out_specs=P("orb", "slab"),
        check_vma=False,
    )
```

```python
import functools

import jax
import jax.numpy as jnp
from jax import lax
from jax.experimental import pallas as pl
from jax.experimental.pallas import tpu as pltpu
from jax.sharding import PartitionSpec as P

HB = 2
EDGE = 2 * HB
GROUP = 8
PLANE = 4
ORDER = (0, 3, 2, 1)
VMEM = pl.BlockSpec(memory_space=pltpu.VMEM)
HBM = pl.BlockSpec(memory_space=pltpu.HBM)
SMEM = pl.BlockSpec(memory_space=pltpu.SMEM)
MIB = 1024 * 1024
f32, bf16 = jnp.float32, jnp.bfloat16


def call(body, limit, out_shape, in_specs, scratch_shapes=(), moved=1000, out_specs=None, **options):
    return pl.pallas_call(
        body,
        out_shape=out_shape,
        in_specs=in_specs,
        out_specs=out_specs or jax.tree.map(lambda _: VMEM, out_shape),
        scratch_shapes=scratch_shapes,
        compiler_params=pltpu.CompilerParams(vmem_limit_bytes=limit * MIB),
        cost_estimate=pl.CostEstimate(flops=1000, bytes_accessed=moved, transcendentals=0),
        **options,
    )


def after(value, *done):
    return lax.optimization_barrier((value, done))[0]


def coefficients(bounds_ref):
    lower_bound = -3.0 + bounds_ref[0]
    cutoff = bounds_ref[1] - 0.5
    upper_bound = 3.0 + bounds_ref[2]
    half_width = (upper_bound - cutoff) / 2.0
    center = (upper_bound + cutoff) / 2.0
    sigma_one = half_width / (lower_bound - center)
    sigma_two = 1.0 / (2.0 / sigma_one - sigma_one)
    first, second, last = sigma_one / half_width, 2.0 * sigma_two / half_width, sigma_one * half_width / 2.0
    return center, first, second, last


def loop(start, stop, body, unroll, carry=0):
    return lax.fori_loop(start, stop, body, carry, unroll=unroll)


def product(tile, block):
    return jnp.dot(tile, block, preferred_element_type=f32)


def is_edge(row, blocks):
    return (row < HB) | (row >= blocks - HB)


def edge_slot(row, blocks):
    return jnp.where(row < HB, row, row - blocks + EDGE)


def edge_row(slot, blocks):
    return slot if slot < HB else blocks - EDGE + slot


def live_mask(tile, lanes, count):
    return lax.broadcasted_iota(jnp.int32, (tile, lanes), 0) < count


def sum_counts(counts_ref, rows):
    total = 0
    for r in rows:
        total = total + counts_ref[r]
    return total


def start_kernel(groups, place_ref, x_ref, rotation_ref, halo_ref, xt_ref, *refs):
    pieces, sems = refs[:-1], refs[-1]
    width = halo_ref.shape[1]
    z, slab, p = place_ref[0], place_ref[1], place_ref[2]
    begin = jnp.where(slab == 0, x_ref.shape[1] - width, 0)
    begin = pl.multiple_of(begin, width)
    copies = [pltpu.make_async_copy(x_ref.at[:, pl.ds(begin, width)], halo_ref, sems.at[0])]
    lanes = pieces[0].shape[1] // groups
    half = groups // 2
    for q, ref in enumerate(pieces):
        for h in range(2):
            for g in range(half):
                block = ((slab ^ h) * half + g) * PLANE + (p ^ q)
                begin = pl.multiple_of(block * lanes, lanes)
                at = (h * half + g) * lanes
                copies.append(
                    pltpu.make_async_copy(
                        rotation_ref.at[:, pl.ds(begin, lanes)],
                        ref.at[:, at:at + lanes],
                        sems.at[len(copies)],
                    )
                )
    for copy in copies:
        copy.start()
    blocks, tile = xt_ref.shape[:2]

    def turn(r, _):
        xt_ref[r] = x_ref[:, pl.ds(pl.multiple_of(r * tile, tile), tile)].T
        return 0

    loop(0, blocks, turn, 16)
    for copy in copies:
        copy.wait()


def multiply(blocks, rows_ref, cols_ref, tiles_ref, source_ref, acc_ref, extra_ref, more):
    def diagonal(r, _):
        acc_ref[r] = product(tiles_ref[r], source_ref[r]) - more(r)
        return 0

    loop(0, blocks, diagonal, 32)
    listed = tiles_ref.shape[0]

    def extra(k, _):
        col = jnp.clip(cols_ref[k], 0, blocks - 1)
        extra_ref[k - blocks] = product(tiles_ref[k], source_ref[col])
        return 0

    loop(blocks, listed, extra, 24)

    def gather(k, _):
        inside = (cols_ref[k] >= 0) & (cols_ref[k] < blocks)
        acc_ref[jnp.where(inside, rows_ref[k], blocks)] += extra_ref[k - blocks]
        return 0

    loop(blocks, listed, gather, 8)


def multiply_edges(blocks, slab, rows_ref, cols_ref, tiles_ref, halo_ref, add):
    def extra(k, _):
        col = cols_ref[k]
        slot = jnp.where(slab == 0, col - blocks, col + HB)

        @pl.when(((col < 0) | (col >= blocks)) & (slot >= 0) & (slot < HB))
        def _():
            add(rows_ref[k], product(tiles_ref[k], halo_ref[slot]))

        return 0

    loop(blocks, tiles_ref.shape[0], extra, 4)


def first_kernel(
    blocks, place_ref, rows_ref, cols_ref, counts_ref, bounds_ref, xt_ref, halo_ref, tiles_ref,
    f1_ref, edge_ref, acc_ref, extra_ref, ext_ref,
):
    tile, lanes = xt_ref.shape[1:]
    slab = place_ref[1]
    center, scale = coefficients(bounds_ref)[:2]

    def more(r):
        return center * xt_ref[r].astype(f32)

    multiply(blocks, rows_ref, cols_ref, tiles_ref, xt_ref, acc_ref, extra_ref, more)
    for b in range(HB):
        ext_ref[b] = halo_ref[:, b * tile:(b + 1) * tile].T

    def add(row, value):
        acc_ref[row] += value

    multiply_edges(blocks, slab, rows_ref, cols_ref, tiles_ref, ext_ref, add)
    def finish(r, _):
        live = live_mask(tile, lanes, counts_ref[r])
        f1_ref[r] = jnp.where(live, acc_ref[r] * scale, 0.0).astype(bf16)
        return 0

    loop(0, blocks, finish, 4)
    begin = jnp.where(slab == 0, blocks - HB, 0)
    for b in range(HB):
        edge_ref[b] = f1_ref[begin + b]


def split_parts(outs, place_ref, packed_ref, base):
    part = outs[0].shape[0]
    for s, out in zip(ORDER, outs):
        start = pl.multiple_of(base + (place_ref[0] ^ s) * part, 16)
        out[...] = packed_ref[pl.ds(start, part)].astype(bf16)


def second_kernel(
    blocks, groups, place_ref, rows_ref, cols_ref, counts_ref, bounds_ref, f1_ref, xt_ref, tiles_ref,
    *refs,
):
    outs, refs = refs[:groups], refs[groups:]
    shared_ref, excess_ref, rest_ref, edge_ref, acc_ref, extra_ref, packed_ref = refs
    tile = tiles_ref.shape[1]
    center, _, scale, last = coefficients(bounds_ref)

    def more(r):
        return center * f1_ref[r].astype(f32) + last * xt_ref[r].astype(f32)

    multiply(blocks, rows_ref, cols_ref, tiles_ref, f1_ref, acc_ref, extra_ref, more)
    edges = [edge_row(e, blocks) for e in range(EDGE)]
    for e, r in enumerate(edges):
        edge_ref[e] = acc_ref[r]
    def finish(r, offset):
        live = live_mask(tile, acc_ref.shape[2], counts_ref[r])
        packed_ref[pl.ds(offset, tile)] = jnp.where(live, acc_ref[r] * scale, 0.0)
        return offset + counts_ref[r]

    loop(HB, blocks - HB, finish, 4, sum_counts(counts_ref, edges))
    size = rest_ref.shape[0]
    rest_ref[...] = packed_ref[:size]
    split_parts(outs, place_ref, packed_ref, size)
    shared_ref[...] = packed_ref[2 * size:3 * size].astype(bf16)
    excess_ref[...] = packed_ref[3 * size:4 * size].astype(bf16)


def second_edge_kernel(
    blocks, groups, place_ref, rows_ref, cols_ref, counts_ref, bounds_ref, halo_ref, tiles_ref,
    sum_ref, rest_ref, *refs,
):
    outs, (acc_ref, packed_ref) = refs[:groups], refs[groups:]
    tile = tiles_ref.shape[1]
    acc_ref[...] = sum_ref[...]

    def add(row, value):
        acc_ref[edge_slot(row, blocks)] += value

    multiply_edges(blocks, place_ref[1], rows_ref, cols_ref, tiles_ref, halo_ref, add)
    scale = coefficients(bounds_ref)[2]
    packed_ref[...] = rest_ref[...]
    offset = 0
    for e in range(EDGE):
        r = edge_row(e, blocks)
        here = pl.ds(offset, tile)
        live = live_mask(tile, acc_ref.shape[2], counts_ref[r])
        packed_ref[here] = jnp.where(live, acc_ref[e] * scale, packed_ref[here])
        offset = offset + counts_ref[r]
    split_parts(outs, place_ref, packed_ref, 0)


def merge_kernel(blocks, groups, place_ref, counts_ref, shared_ref, excess_ref, *refs):
    outs, packed_ref = refs[:groups], refs[groups]
    size = shared_ref.shape[0]
    live = sum_counts(counts_ref, range(blocks))
    packed_ref[:size] = shared_ref[...].astype(f32)
    packed_ref[pl.ds(jnp.clip(live - 2 * size, 0, size), size)] = excess_ref[...].astype(f32)
    split_parts(outs, place_ref, packed_ref, 0)


def rotate_kernel(
    groups, place_ref, own, over_x, core, mine, near, far_two, far_three, other_near, other_ref, *refs
):
    outs, turned = refs[:groups], refs[groups]
    width = outs[0].shape[1]
    half = groups // 2 * width
    lhs = jnp.concatenate(
        [part for s in range(groups) for part in (own[s], core[0, s], over_x[s], core[1, s])], axis=1
    )

    def wide(ref, at=0):
        rows = mine.shape[0]
        return jnp.concatenate(
            [ref[(at + i) * rows:(at + i + 1) * rows] for i in range(groups // 2)], axis=1
        )

    for h in range(2):
        own_half = mine[:, h * half:(h + 1) * half]
        if h == 0:
            rhs = [own_half, near[...], far_two[...], wide(far_three)]
        else:
            rhs = [own_half, other_near[...], wide(other_ref), wide(other_ref, groups // 2)]
        rhs = jnp.concatenate([rhs[s] for s in ORDER], axis=0)
        total = product(lhs, rhs).astype(bf16)
        first = (place_ref[1] ^ h) * (groups // 2)
        for z in range(groups // 2):
            turned[first + z] = total[:, z * width:(z + 1) * width]
    for s, out in zip(ORDER, outs):
        out[...] = turned[place_ref[0] ^ s]


def spread(blocks, tile, counts_ref, cases, block_ref, out_hbm, sems):
    def copy(b):
        there = out_hbm.at[:, pl.ds(pl.multiple_of(b * tile, tile), tile)]
        return pltpu.make_async_copy(block_ref.at[b], there, sems.at[b])

    def each(act):
        def some(g, offset):
            places = []
            for i in range(g * GROUP, (g + 1) * GROUP):
                b = edge_row(i, blocks) if i < EDGE else i - HB
                places.append((b, offset, offset + counts_ref[b]))
                offset = places[-1][2]
            for wanted, source in cases:
                flags = [wanted(begin, end) for _, begin, end in places]

                @pl.when(functools.reduce(jnp.logical_or, flags))
                def _():
                    act(places, flags, source)

            return offset

        offset = 0
        for g in range(blocks // GROUP):
            offset = some(g, offset)

    def write(places, flags, source):
        for b, begin, _ in places:
            rows = source(begin)
            rows = jnp.where(live_mask(tile, rows.shape[1], counts_ref[b]), rows, 0.0).astype(bf16)
            block_ref[b] = rows.T
        for (b, _, _), flag in zip(places, flags):
            @pl.when(flag)
            def _():
                copy(b).start()

    def wait(places, flags, source):
        for (b, _, _), flag in zip(places, flags):
            @pl.when(flag)
            def _():
                copy(b).wait()

    each(write)
    each(wait)


def spread_kernel(blocks, groups, place_ref, counts_ref, *refs):
    parts, (out_hbm, seam_ref, packed_ref, block_ref, sems) = refs[:-5], refs[-5:]
    part = parts[0].shape[0]
    size = part * groups
    tile = block_ref.shape[1]
    for i in range(2):
        for j, s in enumerate(ORDER):
            start = pl.multiple_of((i * groups + (place_ref[0] ^ s)) * part, 16)
            packed_ref[pl.ds(start, part)] = parts[i * groups + j][...].astype(f32)
    seam_ref[0] = packed_ref[:tile]
    seam_ref[1] = packed_ref[2 * size - tile:2 * size]

    def wanted(begin, end):
        return (begin >= size) & (end <= 3 * size)

    def source(begin):
        return packed_ref[pl.ds(jnp.clip(begin - size, 0, 2 * size), tile)]

    spread(blocks, tile, counts_ref, [(wanted, source)], block_ref, out_hbm, sems)


def spread_rest_kernel(blocks, groups, place_ref, counts_ref, done_hbm, seam_ref, back_ref, *refs):
    parts, (out_hbm, packed_ref, far_ref, block_ref, sems) = refs[:-5], refs[-5:]
    part = parts[0].shape[0]
    size = part * groups
    tile = block_ref.shape[1]
    for j, s in enumerate(ORDER):
        start = pl.multiple_of((place_ref[0] ^ s) * part, 16)
        packed_ref[pl.ds(start, part)] = parts[j][...].astype(f32)
    packed_ref[size:] = seam_ref[0]
    live = sum_counts(counts_ref, range(blocks))

    @pl.when(live > 3 * size)
    def _():
        base = jnp.clip(live - 3 * size, 0, size)
        for j, s in enumerate(ORDER):
            far_ref[pl.ds(base + (place_ref[0] ^ s) * part, part)] = back_ref[
                j * part:(j + 1) * part
            ].astype(f32)

    far_ref[size - tile:size] = seam_ref[1]

    def near(begin, end):
        return begin < size

    def near_source(begin):
        return packed_ref[pl.ds(jnp.minimum(begin, size), tile)]

    def far(begin, end):
        return end > 3 * size

    def far_source(begin):
        return far_ref[pl.ds(jnp.clip(begin - 2 * size, 0, 2 * size), tile)]

    cases = [(near, near_source), (far, far_source)]
    spread(blocks, tile, counts_ref, cases, block_ref, out_hbm, sems)


def paired(orbitals_t, tiles, tile_rows, tile_cols, row_counts, bounds, rotation):
    norb_dev, rows_dev = orbitals_t.shape
    listed, tile = tiles.shape[:2]
    blocks = rows_dev // tile
    orbs = lax.axis_size("orb")
    groups = orbs // PLANE
    me, slab = lax.axis_index("orb"), lax.axis_index("slab")
    z, p = me // PLANE, me % PLANE
    place = jnp.stack([z, slab, p])
    size = rows_dev // 4
    part = size // groups
    block_shape = (blocks, tile, norb_dev)
    edge_shape = (EDGE, tile, norb_dev)
    halo_shape = (HB, tile, norb_dev)
    extra_shape = (listed - blocks, tile, norb_dev)
    size_shape = (size, norb_dev)
    lists = (place, tile_rows, tile_cols, row_counts, bounds)

    def shaped(shape, dtype=bf16):
        return jax.ShapeDtypeStruct(shape, dtype)

    part_outs = [shaped((part, norb_dev))] * groups

    def swap(value, bits):
        return lax.ppermute(value, "orb", [(i, i ^ bits) for i in range(orbs)])

    def over_z(values):
        return [swap(v, s * PLANE) if s else v for s, v in zip(ORDER, values)]

    def other_slab(value):
        return lax.ppermute(value, "slab", [(0, 1), (1, 0)])

    half = groups // 2 * norb_dev
    halo, xt, *pieces = call(
        functools.partial(start_kernel, groups),
        20,
        [shaped((norb_dev, HB * tile)), shaped(block_shape)]
        + [shaped((norb_dev, 2 * half))] * PLANE,
        [SMEM, VMEM, HBM],
        [pltpu.SemaphoreType.DMA((1 + PLANE * groups,))],
        moved=20 * MIB,
    )(place, orbitals_t, rotation)
    halo = other_slab(halo)
    mine = [pieces[0]] + [swap(pieces[q], q) for q in range(1, PLANE)]
    mine = jnp.concatenate(after(mine, halo), axis=0)
    far_two = swap(mine[:, :half], 2 * PLANE)
    near = swap(mine[:, :half], PLANE)
    f1, edge = call(
        functools.partial(first_kernel, blocks),
        16,
        [shaped(block_shape), shaped(halo_shape)],
        [SMEM] * 5 + [VMEM] * 3,
        [
            pltpu.VMEM((blocks + 1, tile, norb_dev), f32),
            pltpu.VMEM(extra_shape, f32),
            pltpu.VMEM(halo_shape, bf16),
        ],
    )(*lists, xt, halo, tiles)
    halo = other_slab(edge)

    *first_parts, shared, excess, rest, edge_sum = call(
        functools.partial(second_kernel, blocks, groups),
        18,
        part_outs
        + [shaped(size_shape)] * 2 + [shaped(size_shape, f32), shaped(edge_shape, f32)],
        [SMEM] * 5 + [VMEM] * 3,
        [
            pltpu.VMEM((blocks + 1, tile, norb_dev), f32),
            pltpu.VMEM(extra_shape, f32),
            pltpu.VMEM((rows_dev + tile, norb_dev), f32),
        ],
    )(*lists, f1, xt, tiles)

    def together(*values):
        return lax.optimization_barrier(values)

    def over_core(own, over_x):
        return swap(jnp.stack([own, over_x]), 1)

    def rotate(*gathered):
        return call(
            functools.partial(rotate_kernel, groups),
            12,
            part_outs,
            [SMEM] + [VMEM] * (3 + len(weights)),
            [pltpu.VMEM((groups, part, norb_dev), bf16)],
        )(place, *gathered, *weights)

    excess, halo, first_parts, near, far_two = together(excess, halo, first_parts, near, far_two)
    excess = other_slab(excess)
    other_near = other_slab(near)
    columns = [far_two[:, i * norb_dev:(i + 1) * norb_dev] for i in range(groups // 2)]
    first_parts = list(first_parts)
    nearest = ORDER.index(1)
    first_parts[nearest] = jnp.concatenate([first_parts[nearest]] + columns)
    first = over_z(first_parts)
    shared_parts = call(
        functools.partial(merge_kernel, blocks, groups),
        8,
        part_outs,
        [SMEM] * 2 + [VMEM] * 2,
        [pltpu.VMEM((2 * size, norb_dev), f32)],
    )(place, row_counts, shared, excess)

    first, shared_parts, rest, other_near = together(first, shared_parts, rest, other_near)
    far_three, first[nearest] = first[nearest][part:], first[nearest][:part]
    shared = over_z(shared_parts)
    first_own = jnp.stack(first)
    first_x = swap(first_own, 2)
    others = other_slab(jnp.concatenate(columns + [far_three]))
    rest_parts = call(
        functools.partial(second_edge_kernel, blocks, groups),
        8,
        part_outs,
        [SMEM] * 5 + [VMEM] * 4,
        [pltpu.VMEM(edge_shape, f32), pltpu.VMEM(size_shape, f32)],
    )(*lists, halo, tiles, edge_sum, rest)

    shared, first_x, rest_parts, others = together(shared, first_x, rest_parts, others)
    rest = over_z(rest_parts)
    first_core = over_core(first_own, first_x)
    shared_own = jnp.stack(shared)
    shared_x = swap(shared_own, 2)
    weights = [mine, near, far_two, far_three, other_near, others]
    first_turned = rotate(first_own, first_x, first_core)

    rest, first_turned, shared_x = together(rest, first_turned, shared_x)
    first_back = over_z(first_turned)
    shared_core = over_core(shared_own, shared_x)
    rest_own = jnp.stack(rest)
    rest_x = swap(rest_own, 2)
    shared_turned = rotate(shared_own, shared_x, shared_core)

    first_back, shared_turned, rest_x = together(first_back, shared_turned, rest_x)
    shared_back = over_z(shared_turned)
    rest_core = over_core(rest_own, rest_x)
    rest_turned = rotate(rest_own, rest_x, rest_core)

    shared_back, rest_turned = together(shared_back, rest_turned)
    rest_back = over_z(rest_turned)
    back = other_slab(jnp.concatenate(shared_back))
    width_shape = (blocks, norb_dev, tile)
    out = shaped((norb_dev, rows_dev))
    done, seam = call(
        functools.partial(spread_kernel, blocks, groups),
        12,
        [out, shaped((2, tile, norb_dev), f32)],
        [SMEM] * 2 + [VMEM] * (2 * groups),
        [
            pltpu.VMEM((2 * size + tile, norb_dev), f32),
            pltpu.VMEM(width_shape, bf16),
            pltpu.SemaphoreType.DMA((blocks,)),
        ],
        out_specs=[HBM, VMEM],
    )(place, row_counts, *first_back, *shared_back)
    return call(
        functools.partial(spread_rest_kernel, blocks, groups),
        12,
        out,
        [SMEM] * 2 + [HBM] + [VMEM] * (2 + groups),
        [
            pltpu.VMEM((size + tile, norb_dev), f32),
            pltpu.VMEM((2 * size + tile, norb_dev), f32),
            pltpu.VMEM(width_shape, bf16),
            pltpu.SemaphoreType.DMA((blocks,)),
        ],
        out_specs=HBM,
        input_output_aliases={2: 0},
    )(place, row_counts, done, seam, back, *rest_back)


def with_halo(block, sides, width):
    for axis, dim in sides:
        count = lax.axis_size(axis)
        forward = [(i, i + 1) for i in range(count - 1)]
        backward = [(target, source) for source, target in forward]
        low = lax.ppermute(
            lax.slice_in_dim(block, block.shape[dim] - width, None, axis=dim), axis, forward
        )
        high = lax.ppermute(lax.slice_in_dim(block, 0, width, axis=dim), axis, backward)
        block = jnp.concatenate([low, block, high], axis=dim)
    return block


def general(orbitals_t, tiles, tile_rows, tile_cols, row_counts, bounds, rotation):
    norb_dev, rows_dev = orbitals_t.shape
    tile_size = tiles.shape[1]
    blocks = rows_dev // tile_size
    lower_bound = -3.0 + bounds[0]
    cutoff = bounds[1] - 0.5
    upper_bound = 3.0 + bounds[2]
    half_width = (upper_bound - cutoff) / 2.0
    center = (upper_bound + cutoff) / 2.0
    sigma_one = half_width / (lower_bound - center)
    sigma_two = 1.0 / (2.0 / sigma_one - sigma_one)
    live = (
        (lax.broadcasted_iota(jnp.int32, (blocks, tile_size), 1) < row_counts[:, None])
        .astype(jnp.float32)
        .reshape(rows_dev)
    )
    extra_rows = tile_rows[blocks:]
    onehot = (extra_rows[:, None] == lax.broadcasted_iota(jnp.int32, (1, blocks), 1)).astype(
        jnp.float32
    )
    col_index = tile_cols + HB

    def apply_tiles(source):
        extended = with_halo(source, (("slab", 1),), HB * tile_size)
        col_blocks = extended.reshape(norb_dev, blocks + 2 * HB, tile_size)
        picked = jnp.take(col_blocks, col_index, axis=1)
        products = jnp.einsum("otc,trc->otr", picked, tiles, preferred_element_type=jnp.float32)
        diagonal_part = products[:, :blocks]
        extra_part = jnp.einsum(
            "otr,tb->obr", products[:, blocks:], onehot, precision=lax.Precision.HIGH
        )
        summed = diagonal_part + extra_part
        return summed.reshape(norb_dev, rows_dev)

    source = orbitals_t.astype(jnp.float32)
    applied = apply_tiles(orbitals_t)
    filtered_one = (live * (applied - center * source) * (sigma_one / half_width)).astype(
        jnp.bfloat16
    )
    applied = apply_tiles(filtered_one)
    first = filtered_one.astype(jnp.float32)
    filtered_two = (
        live
        * (
            (applied - center * first) * (2.0 * sigma_two / half_width)
            - sigma_one * sigma_two * source
        )
    ).astype(jnp.bfloat16)
    row_major = lax.all_to_all(filtered_two, "orb", split_axis=1, concat_axis=0, tiled=True)
    rotated = jnp.einsum(
        "kj,kr->jr",
        lax.all_gather(rotation, "orb", axis=0, tiled=True),
        row_major,
        preferred_element_type=jnp.float32,
    ).astype(jnp.bfloat16)
    return lax.all_to_all(rotated, "orb", split_axis=0, concat_axis=1, tiled=True)


def local(orbitals_t, tiles, *rest):
    slabs, orbs = lax.axis_size("slab"), lax.axis_size("orb")
    fits = slabs == 2 and orbs == PLANE * PLANE and orbitals_t.shape[0] % tiles.shape[1] == 0
    return (paired if fits else general)(orbitals_t, tiles, *rest)


def solution(mesh):
    return jax.shard_map(
        local,
        mesh=mesh,
        in_specs=(
            P("orb", "slab"),
            P("slab", None, None),
            P("slab"),
            P("slab"),
            P("slab"),
            P(),
            P("orb", None),
        ),
        out_specs=P("orb", "slab"),
        check_vma=False,
    )
```

```python
import functools

import jax
import jax.numpy as jnp
from jax import lax
from jax.experimental import pallas as pl
from jax.experimental.pallas import tpu as pltpu
from jax.sharding import PartitionSpec as P

HB = 2
EDGE = 2 * HB
GROUP = 4
PLANE = 4
ORDER = (0, 3, 2, 1)
VMEM = pl.BlockSpec(memory_space=pltpu.VMEM)
HBM = pl.BlockSpec(memory_space=pltpu.HBM)
SMEM = pl.BlockSpec(memory_space=pltpu.SMEM)
MIB = 1024 * 1024
f32, bf16 = jnp.float32, jnp.bfloat16


def call(body, limit, out_shape, in_specs, scratch_shapes=(), moved=1000, out_specs=None, **options):
    return pl.pallas_call(
        body,
        out_shape=out_shape,
        in_specs=in_specs,
        out_specs=out_specs or jax.tree.map(lambda _: VMEM, out_shape),
        scratch_shapes=scratch_shapes,
        compiler_params=pltpu.CompilerParams(vmem_limit_bytes=limit * MIB),
        cost_estimate=pl.CostEstimate(flops=1000, bytes_accessed=moved, transcendentals=0),
        **options,
    )


def after(value, *done):
    return lax.optimization_barrier((value, done))[0]


def coefficients(bounds_ref):
    lower_bound = -3.0 + bounds_ref[0]
    cutoff = bounds_ref[1] - 0.5
    upper_bound = 3.0 + bounds_ref[2]
    half_width = (upper_bound - cutoff) / 2.0
    center = (upper_bound + cutoff) / 2.0
    sigma_one = half_width / (lower_bound - center)
    sigma_two = 1.0 / (2.0 / sigma_one - sigma_one)
    first, second, last = sigma_one / half_width, 2.0 * sigma_two / half_width, sigma_one * half_width / 2.0
    return center, first, second, last


def loop(start, stop, body, unroll, carry=0):
    return lax.fori_loop(start, stop, body, carry, unroll=unroll)


def product(tile, block):
    return jnp.dot(tile, block, preferred_element_type=f32)


def is_edge(row, blocks):
    return (row < HB) | (row >= blocks - HB)


def edge_slot(row, blocks):
    return jnp.where(row < HB, row, row - blocks + EDGE)


def edge_row(slot, blocks):
    return slot if slot < HB else blocks - EDGE + slot


def live_mask(tile, lanes, count):
    return lax.broadcasted_iota(jnp.int32, (tile, lanes), 0) < count


def sum_counts(counts_ref, rows):
    total = 0
    for r in rows:
        total = total + counts_ref[r]
    return total


def start_kernel(groups, place_ref, x_ref, rotation_ref, halo_ref, xt_ref, *refs):
    pieces, sems = refs[:-1], refs[-1]
    width = halo_ref.shape[1]
    z, slab, p = place_ref[0], place_ref[1], place_ref[2]
    begin = jnp.where(slab == 0, x_ref.shape[1] - width, 0)
    begin = pl.multiple_of(begin, width)
    copies = [pltpu.make_async_copy(x_ref.at[:, pl.ds(begin, width)], halo_ref, sems.at[0])]
    lanes = pieces[0].shape[1] // groups
    half = groups // 2
    for q, ref in enumerate(pieces):
        for h in range(2):
            for g in range(half):
                block = ((slab ^ h) * half + g) * PLANE + (p ^ q)
                begin = pl.multiple_of(block * lanes, lanes)
                at = (h * half + g) * lanes
                copies.append(
                    pltpu.make_async_copy(
                        rotation_ref.at[:, pl.ds(begin, lanes)],
                        ref.at[:, at:at + lanes],
                        sems.at[len(copies)],
                    )
                )
    for copy in copies:
        copy.start()
    blocks, tile = xt_ref.shape[:2]

    def turn(r, _):
        xt_ref[r] = x_ref[:, pl.ds(pl.multiple_of(r * tile, tile), tile)].T
        return 0

    loop(0, blocks, turn, 16)
    for copy in copies:
        copy.wait()


def multiply(blocks, rows_ref, cols_ref, tiles_ref, source_ref, acc_ref, extra_ref, more):
    def diagonal(r, _):
        acc_ref[r] = product(tiles_ref[r], source_ref[r]) - more(r)
        return 0

    loop(0, blocks, diagonal, 32)
    listed = tiles_ref.shape[0]

    def extra(k, _):
        col = jnp.clip(cols_ref[k], 0, blocks - 1)
        extra_ref[k - blocks] = product(tiles_ref[k], source_ref[col])
        return 0

    loop(blocks, listed, extra, 24)

    def gather(k, _):
        inside = (cols_ref[k] >= 0) & (cols_ref[k] < blocks)
        acc_ref[jnp.where(inside, rows_ref[k], blocks)] += extra_ref[k - blocks]
        return 0

    loop(blocks, listed, gather, 8)


def multiply_edges(blocks, slab, rows_ref, cols_ref, tiles_ref, halo_ref, add):
    def extra(k, _):
        col = cols_ref[k]
        slot = jnp.where(slab == 0, col - blocks, col + HB)

        @pl.when(((col < 0) | (col >= blocks)) & (slot >= 0) & (slot < HB))
        def _():
            add(rows_ref[k], product(tiles_ref[k], halo_ref[slot]))

        return 0

    loop(blocks, tiles_ref.shape[0], extra, 4)


def first_kernel(
    blocks, place_ref, rows_ref, cols_ref, counts_ref, bounds_ref, xt_ref, halo_ref, tiles_ref,
    f1_ref, edge_ref, acc_ref, extra_ref, ext_ref,
):
    tile, lanes = xt_ref.shape[1:]
    slab = place_ref[1]
    center, scale = coefficients(bounds_ref)[:2]

    def more(r):
        return center * xt_ref[r].astype(f32)

    multiply(blocks, rows_ref, cols_ref, tiles_ref, xt_ref, acc_ref, extra_ref, more)
    for b in range(HB):
        ext_ref[b] = halo_ref[:, b * tile:(b + 1) * tile].T

    def add(row, value):
        acc_ref[row] += value

    multiply_edges(blocks, slab, rows_ref, cols_ref, tiles_ref, ext_ref, add)
    def finish(r, _):
        live = live_mask(tile, lanes, counts_ref[r])
        f1_ref[r] = jnp.where(live, acc_ref[r] * scale, 0.0).astype(bf16)
        return 0

    loop(0, blocks, finish, 4)
    begin = jnp.where(slab == 0, blocks - HB, 0)
    for b in range(HB):
        edge_ref[b] = f1_ref[begin + b]


def split_parts(outs, place_ref, packed_ref, base):
    part = outs[0].shape[0]
    for s, out in zip(ORDER, outs):
        start = pl.multiple_of(base + (place_ref[0] ^ s) * part, 16)
        out[...] = packed_ref[pl.ds(start, part)].astype(bf16)


def second_kernel(
    blocks, groups, place_ref, rows_ref, cols_ref, counts_ref, bounds_ref, f1_ref, xt_ref, tiles_ref,
    *refs,
):
    outs, refs = refs[:groups], refs[groups:]
    shared_ref, excess_ref, rest_ref, edge_ref, acc_ref, extra_ref, packed_ref = refs
    tile = tiles_ref.shape[1]
    center, _, scale, last = coefficients(bounds_ref)

    def more(r):
        return center * f1_ref[r].astype(f32) + last * xt_ref[r].astype(f32)

    multiply(blocks, rows_ref, cols_ref, tiles_ref, f1_ref, acc_ref, extra_ref, more)
    edges = [edge_row(e, blocks) for e in range(EDGE)]
    for e, r in enumerate(edges):
        edge_ref[e] = acc_ref[r]
    def finish(r, offset):
        live = live_mask(tile, acc_ref.shape[2], counts_ref[r])
        packed_ref[pl.ds(offset, tile)] = jnp.where(live, acc_ref[r] * scale, 0.0)
        return offset + counts_ref[r]

    loop(HB, blocks - HB, finish, 4, sum_counts(counts_ref, edges))
    size = rest_ref.shape[0]
    rest_ref[...] = packed_ref[:size]
    split_parts(outs, place_ref, packed_ref, size)
    shared_ref[...] = packed_ref[2 * size:3 * size].astype(bf16)
    excess_ref[...] = packed_ref[3 * size:4 * size].astype(bf16)


def second_edge_kernel(
    blocks, groups, place_ref, rows_ref, cols_ref, counts_ref, bounds_ref, halo_ref, tiles_ref,
    sum_ref, rest_ref, *refs,
):
    outs, (acc_ref, packed_ref) = refs[:groups], refs[groups:]
    tile = tiles_ref.shape[1]
    acc_ref[...] = sum_ref[...]

    def add(row, value):
        acc_ref[edge_slot(row, blocks)] += value

    multiply_edges(blocks, place_ref[1], rows_ref, cols_ref, tiles_ref, halo_ref, add)
    scale = coefficients(bounds_ref)[2]
    packed_ref[...] = rest_ref[...]
    offset = 0
    for e in range(EDGE):
        r = edge_row(e, blocks)
        here = pl.ds(offset, tile)
        live = live_mask(tile, acc_ref.shape[2], counts_ref[r])
        packed_ref[here] = jnp.where(live, acc_ref[e] * scale, packed_ref[here])
        offset = offset + counts_ref[r]
    split_parts(outs, place_ref, packed_ref, 0)


def merge_kernel(blocks, groups, place_ref, counts_ref, shared_ref, excess_ref, *refs):
    outs, packed_ref = refs[:groups], refs[groups]
    size = shared_ref.shape[0]
    live = sum_counts(counts_ref, range(blocks))
    packed_ref[:size] = shared_ref[...].astype(f32)
    packed_ref[pl.ds(jnp.clip(live - 2 * size, 0, size), size)] = excess_ref[...].astype(f32)
    split_parts(outs, place_ref, packed_ref, 0)


def rotate_kernel(
    groups, place_ref, own, over_x, core, mine, near, far_two, far_three, other_near, other_ref, *refs
):
    outs, turned = refs[:groups], refs[groups]
    width = outs[0].shape[1]
    half = groups // 2 * width
    lhs = jnp.concatenate(
        [part for s in range(groups) for part in (own[s], core[0, s], over_x[s], core[1, s])], axis=1
    )

    def wide(ref, at=0):
        rows = mine.shape[0]
        return jnp.concatenate(
            [ref[(at + i) * rows:(at + i + 1) * rows] for i in range(groups // 2)], axis=1
        )

    for h in range(2):
        own_half = mine[:, h * half:(h + 1) * half]
        if h == 0:
            rhs = [own_half, near[...], far_two[...], wide(far_three)]
        else:
            rhs = [own_half, other_near[...], wide(other_ref), wide(other_ref, groups // 2)]
        rhs = jnp.concatenate([rhs[s] for s in ORDER], axis=0)
        total = product(lhs, rhs).astype(bf16)
        first = (place_ref[1] ^ h) * (groups // 2)
        for z in range(groups // 2):
            turned[first + z] = total[:, z * width:(z + 1) * width]
    for s, out in zip(ORDER, outs):
        out[...] = turned[place_ref[0] ^ s]


def spread(blocks, tile, counts_ref, cases, block_ref, out_hbm, sems):
    def copy(b):
        there = out_hbm.at[:, pl.ds(pl.multiple_of(b * tile, tile), tile)]
        return pltpu.make_async_copy(block_ref.at[b], there, sems.at[b])

    def each(act):
        def some(g, offset):
            places = []
            for i in range(g * GROUP, (g + 1) * GROUP):
                b = edge_row(i, blocks) if i < EDGE else i - HB
                places.append((b, offset, offset + counts_ref[b]))
                offset = places[-1][2]
            for wanted, source in cases:
                flags = [wanted(begin, end) for _, begin, end in places]

                @pl.when(functools.reduce(jnp.logical_or, flags))
                def _():
                    act(places, flags, source)

            return offset

        offset = 0
        for g in range(blocks // GROUP):
            offset = some(g, offset)

    def write(places, flags, source):
        for b, begin, _ in places:
            rows = source(begin)
            rows = jnp.where(live_mask(tile, rows.shape[1], counts_ref[b]), rows, 0.0).astype(bf16)
            block_ref[b] = rows.T
        for (b, _, _), flag in zip(places, flags):
            @pl.when(flag)
            def _():
                copy(b).start()

    def wait(places, flags, source):
        for (b, _, _), flag in zip(places, flags):
            @pl.when(flag)
            def _():
                copy(b).wait()

    each(write)
    each(wait)


def spread_kernel(blocks, groups, place_ref, counts_ref, *refs):
    parts, (out_hbm, seam_ref, packed_ref, block_ref, sems) = refs[:-5], refs[-5:]
    part = parts[0].shape[0]
    size = part * groups
    tile = block_ref.shape[1]
    for i in range(2):
        for j, s in enumerate(ORDER):
            start = pl.multiple_of((i * groups + (place_ref[0] ^ s)) * part, 16)
            packed_ref[pl.ds(start, part)] = parts[i * groups + j][...].astype(f32)
    seam_ref[0] = packed_ref[:tile]
    seam_ref[1] = packed_ref[2 * size - tile:2 * size]

    def wanted(begin, end):
        return (begin >= size) & (end <= 3 * size)

    def source(begin):
        return packed_ref[pl.ds(jnp.clip(begin - size, 0, 2 * size), tile)]

    spread(blocks, tile, counts_ref, [(wanted, source)], block_ref, out_hbm, sems)


def spread_rest_kernel(blocks, groups, place_ref, counts_ref, done_hbm, seam_ref, back_ref, *refs):
    parts, (out_hbm, packed_ref, far_ref, block_ref, sems) = refs[:-5], refs[-5:]
    part = parts[0].shape[0]
    size = part * groups
    tile = block_ref.shape[1]
    for j, s in enumerate(ORDER):
        start = pl.multiple_of((place_ref[0] ^ s) * part, 16)
        packed_ref[pl.ds(start, part)] = parts[j][...].astype(f32)
    packed_ref[size:] = seam_ref[0]
    live = sum_counts(counts_ref, range(blocks))

    @pl.when(live > 3 * size)
    def _():
        base = jnp.clip(live - 3 * size, 0, size)
        for j, s in enumerate(ORDER):
            far_ref[pl.ds(base + (place_ref[0] ^ s) * part, part)] = back_ref[
                j * part:(j + 1) * part
            ].astype(f32)

    far_ref[size - tile:size] = seam_ref[1]

    def near(begin, end):
        return begin < size

    def near_source(begin):
        return packed_ref[pl.ds(jnp.minimum(begin, size), tile)]

    def far(begin, end):
        return end > 3 * size

    def far_source(begin):
        return far_ref[pl.ds(jnp.clip(begin - 2 * size, 0, 2 * size), tile)]

    cases = [(near, near_source), (far, far_source)]
    spread(blocks, tile, counts_ref, cases, block_ref, out_hbm, sems)


def paired(orbitals_t, tiles, tile_rows, tile_cols, row_counts, bounds, rotation):
    norb_dev, rows_dev = orbitals_t.shape
    listed, tile = tiles.shape[:2]
    blocks = rows_dev // tile
    orbs = lax.axis_size("orb")
    groups = orbs // PLANE
    me, slab = lax.axis_index("orb"), lax.axis_index("slab")
    z, p = me // PLANE, me % PLANE
    place = jnp.stack([z, slab, p])
    size = rows_dev // 4
    part = size // groups
    block_shape = (blocks, tile, norb_dev)
    edge_shape = (EDGE, tile, norb_dev)
    halo_shape = (HB, tile, norb_dev)
    extra_shape = (listed - blocks, tile, norb_dev)
    size_shape = (size, norb_dev)
    lists = (place, tile_rows, tile_cols, row_counts, bounds)

    def shaped(shape, dtype=bf16):
        return jax.ShapeDtypeStruct(shape, dtype)

    part_outs = [shaped((part, norb_dev))] * groups

    def swap(value, bits):
        return lax.ppermute(value, "orb", [(i, i ^ bits) for i in range(orbs)])

    def over_z(values):
        return [swap(v, s * PLANE) if s else v for s, v in zip(ORDER, values)]

    def other_slab(value):
        return lax.ppermute(value, "slab", [(0, 1), (1, 0)])

    half = groups // 2 * norb_dev
    halo, xt, *pieces = call(
        functools.partial(start_kernel, groups),
        20,
        [shaped((norb_dev, HB * tile)), shaped(block_shape)]
        + [shaped((norb_dev, 2 * half))] * PLANE,
        [SMEM, VMEM, HBM],
        [pltpu.SemaphoreType.DMA((1 + PLANE * groups,))],
        moved=20 * MIB,
    )(place, orbitals_t, rotation)
    halo = other_slab(halo)
    mine = [pieces[0]] + [swap(pieces[q], q) for q in range(1, PLANE)]
    mine = jnp.concatenate(after(mine, halo), axis=0)
    far_two = swap(mine[:, :half], 2 * PLANE)
    near = swap(mine[:, :half], PLANE)
    f1, edge = call(
        functools.partial(first_kernel, blocks),
        16,
        [shaped(block_shape), shaped(halo_shape)],
        [SMEM] * 5 + [VMEM] * 3,
        [
            pltpu.VMEM((blocks + 1, tile, norb_dev), f32),
            pltpu.VMEM(extra_shape, f32),
            pltpu.VMEM(halo_shape, bf16),
        ],
    )(*lists, xt, halo, tiles)
    halo = other_slab(edge)

    *first_parts, shared, excess, rest, edge_sum = call(
        functools.partial(second_kernel, blocks, groups),
        18,
        part_outs
        + [shaped(size_shape)] * 2 + [shaped(size_shape, f32), shaped(edge_shape, f32)],
        [SMEM] * 5 + [VMEM] * 3,
        [
            pltpu.VMEM((blocks + 1, tile, norb_dev), f32),
            pltpu.VMEM(extra_shape, f32),
            pltpu.VMEM((rows_dev + tile, norb_dev), f32),
        ],
    )(*lists, f1, xt, tiles)

    def together(*values):
        return lax.optimization_barrier(values)

    def over_core(own, over_x):
        return swap(jnp.stack([own, over_x]), 1)

    def rotate(*gathered):
        return call(
            functools.partial(rotate_kernel, groups),
            12,
            part_outs,
            [SMEM] + [VMEM] * (3 + len(weights)),
            [pltpu.VMEM((groups, part, norb_dev), bf16)],
        )(place, *gathered, *weights)

    excess, halo, first_parts, near, far_two = together(excess, halo, first_parts, near, far_two)
    excess = other_slab(excess)
    other_near = other_slab(near)
    columns = [far_two[:, i * norb_dev:(i + 1) * norb_dev] for i in range(groups // 2)]
    first_parts = list(first_parts)
    nearest = ORDER.index(1)
    first_parts[nearest] = jnp.concatenate([first_parts[nearest]] + columns)
    first = over_z(first_parts)
    shared_parts = call(
        functools.partial(merge_kernel, blocks, groups),
        8,
        part_outs,
        [SMEM] * 2 + [VMEM] * 2,
        [pltpu.VMEM((2 * size, norb_dev), f32)],
    )(place, row_counts, shared, excess)

    first, shared_parts, rest, other_near = together(first, shared_parts, rest, other_near)
    far_three, first[nearest] = first[nearest][part:], first[nearest][:part]
    shared = over_z(shared_parts)
    first_own = jnp.stack(first)
    first_x = swap(first_own, 2)
    others = other_slab(jnp.concatenate(columns + [far_three]))
    rest_parts = call(
        functools.partial(second_edge_kernel, blocks, groups),
        8,
        part_outs,
        [SMEM] * 5 + [VMEM] * 4,
        [pltpu.VMEM(edge_shape, f32), pltpu.VMEM(size_shape, f32)],
    )(*lists, halo, tiles, edge_sum, rest)

    shared, first_x, rest_parts, others = together(shared, first_x, rest_parts, others)
    rest = over_z(rest_parts)
    first_core = over_core(first_own, first_x)
    shared_own = jnp.stack(shared)
    shared_x = swap(shared_own, 2)
    weights = [mine, near, far_two, far_three, other_near, others]
    first_turned = rotate(first_own, first_x, first_core)

    rest, first_turned, shared_x = together(rest, first_turned, shared_x)
    first_back = over_z(first_turned)
    shared_core = over_core(shared_own, shared_x)
    rest_own = jnp.stack(rest)
    rest_x = swap(rest_own, 2)
    shared_turned = rotate(shared_own, shared_x, shared_core)

    first_back, shared_turned, rest_x = together(first_back, shared_turned, rest_x)
    shared_back = over_z(shared_turned)
    rest_core = over_core(rest_own, rest_x)
    rest_turned = rotate(rest_own, rest_x, rest_core)

    shared_back, rest_turned = together(shared_back, rest_turned)
    rest_back = over_z(rest_turned)
    back = other_slab(jnp.concatenate(shared_back))
    width_shape = (blocks, norb_dev, tile)
    out = shaped((norb_dev, rows_dev))
    done, seam = call(
        functools.partial(spread_kernel, blocks, groups),
        12,
        [out, shaped((2, tile, norb_dev), f32)],
        [SMEM] * 2 + [VMEM] * (2 * groups),
        [
            pltpu.VMEM((2 * size + tile, norb_dev), f32),
            pltpu.VMEM(width_shape, bf16),
            pltpu.SemaphoreType.DMA((blocks,)),
        ],
        out_specs=[HBM, VMEM],
    )(place, row_counts, *first_back, *shared_back)
    return call(
        functools.partial(spread_rest_kernel, blocks, groups),
        12,
        out,
        [SMEM] * 2 + [HBM] + [VMEM] * (2 + groups),
        [
            pltpu.VMEM((size + tile, norb_dev), f32),
            pltpu.VMEM((2 * size + tile, norb_dev), f32),
            pltpu.VMEM(width_shape, bf16),
            pltpu.SemaphoreType.DMA((blocks,)),
        ],
        out_specs=HBM,
        input_output_aliases={2: 0},
    )(place, row_counts, done, seam, back, *rest_back)


def with_halo(block, sides, width):
    for axis, dim in sides:
        count = lax.axis_size(axis)
        forward = [(i, i + 1) for i in range(count - 1)]
        backward = [(target, source) for source, target in forward]
        low = lax.ppermute(
            lax.slice_in_dim(block, block.shape[dim] - width, None, axis=dim), axis, forward
        )
        high = lax.ppermute(lax.slice_in_dim(block, 0, width, axis=dim), axis, backward)
        block = jnp.concatenate([low, block, high], axis=dim)
    return block


def general(orbitals_t, tiles, tile_rows, tile_cols, row_counts, bounds, rotation):
    norb_dev, rows_dev = orbitals_t.shape
    tile_size = tiles.shape[1]
    blocks = rows_dev // tile_size
    lower_bound = -3.0 + bounds[0]
    cutoff = bounds[1] - 0.5
    upper_bound = 3.0 + bounds[2]
    half_width = (upper_bound - cutoff) / 2.0
    center = (upper_bound + cutoff) / 2.0
    sigma_one = half_width / (lower_bound - center)
    sigma_two = 1.0 / (2.0 / sigma_one - sigma_one)
    live = (
        (lax.broadcasted_iota(jnp.int32, (blocks, tile_size), 1) < row_counts[:, None])
        .astype(jnp.float32)
        .reshape(rows_dev)
    )
    extra_rows = tile_rows[blocks:]
    onehot = (extra_rows[:, None] == lax.broadcasted_iota(jnp.int32, (1, blocks), 1)).astype(
        jnp.float32
    )
    col_index = tile_cols + HB

    def apply_tiles(source):
        extended = with_halo(source, (("slab", 1),), HB * tile_size)
        col_blocks = extended.reshape(norb_dev, blocks + 2 * HB, tile_size)
        picked = jnp.take(col_blocks, col_index, axis=1)
        products = jnp.einsum("otc,trc->otr", picked, tiles, preferred_element_type=jnp.float32)
        diagonal_part = products[:, :blocks]
        extra_part = jnp.einsum(
            "otr,tb->obr", products[:, blocks:], onehot, precision=lax.Precision.HIGH
        )
        summed = diagonal_part + extra_part
        return summed.reshape(norb_dev, rows_dev)

    source = orbitals_t.astype(jnp.float32)
    applied = apply_tiles(orbitals_t)
    filtered_one = (live * (applied - center * source) * (sigma_one / half_width)).astype(
        jnp.bfloat16
    )
    applied = apply_tiles(filtered_one)
    first = filtered_one.astype(jnp.float32)
    filtered_two = (
        live
        * (
            (applied - center * first) * (2.0 * sigma_two / half_width)
            - sigma_one * sigma_two * source
        )
    ).astype(jnp.bfloat16)
    row_major = lax.all_to_all(filtered_two, "orb", split_axis=1, concat_axis=0, tiled=True)
    rotated = jnp.einsum(
        "kj,kr->jr",
        lax.all_gather(rotation, "orb", axis=0, tiled=True),
        row_major,
        preferred_element_type=jnp.float32,
    ).astype(jnp.bfloat16)
    return lax.all_to_all(rotated, "orb", split_axis=0, concat_axis=1, tiled=True)


def local(orbitals_t, tiles, *rest):
    slabs, orbs = lax.axis_size("slab"), lax.axis_size("orb")
    fits = slabs == 2 and orbs == PLANE * PLANE and orbitals_t.shape[0] % tiles.shape[1] == 0
    return (paired if fits else general)(orbitals_t, tiles, *rest)


def solution(mesh):
    return jax.shard_map(
        local,
        mesh=mesh,
        in_specs=(
            P("orb", "slab"),
            P("slab", None, None),
            P("slab"),
            P("slab"),
            P("slab"),
            P(),
            P("orb", None),
        ),
        out_specs=P("orb", "slab"),
        check_vma=False,
    )
```
